32 devices in a mesh: dp: 16 (over z, y, x), tensor: 2 (over core).
Axes of the slice: x: 2, y: 2, z: 4, core: 2. Of those that a mesh axis runs over, the one named last changes fastest.
Arguments:
- gradient: bfloat16 [16, 256, 3584], P('dp', 'tensor'), may hold values from -84 to 84
- thresholds: int32 [16, 256, 3584], P('dp', 'tensor'), may hold values from 0 to 4095
- sign_bits: int32 [3584], replicated, may hold values 0 or 1
- levels: int32 [16], replicated, may hold values from 0 to 36, as said below
- clip_rms: float32 [1], replicated, may hold values from 0.5 to 1
Outputs:
- summed_grad: bfloat16 [256, 3584], P('tensor')
The draws below stay inside these ranges and needn't reach their ends.
Inputs may be any that keep to these rules, and one draw needn't show every extreme that they name: levels[0] is 0, the entries rise strictly by 1 to 4 from one to the next, and levels[15] is the promised most.
All inputs are finite; a program needn't handle non-finite values.
Results may differ from the reference program's by a relative error of at most 0.0004.
Values may be sent and summed in bfloat16 or wider, within the bound.
A program may use at most 64 MiB of HBM per device.

```python
import math
import jax
import jax.numpy as jnp
from jax import lax

D = 3584
BLOCK = 128
LEVELS = 16
ROWS = 256
REPLICAS = 16


def draw_gradient(key, part):
    key = jax.random.fold_in(key, 1)
    keys = jax.random.split(key, 5)
    ramp = jnp.arange(ROWS, dtype=jnp.float32) / ROWS
    row_scale = jnp.exp(math.log(10.0) * ramp) * jax.random.uniform(keys[0], (ROWS,), jnp.float32, 0.7, 1.4)
    col_scale = jnp.exp(math.log(10.0) * jax.random.uniform(keys[1], (D,), jnp.float32))
    values = jax.random.normal(keys[4], (REPLICAS, ROWS, D), jnp.float32)
    values = jnp.clip(values, -6.0, 6.0)
    return (0.1 * values * row_scale[None, :, None] * col_scale[None, None, :]).astype(jnp.bfloat16)


def draw_levels(key, part):
    key = jax.random.fold_in(key, 2)
    step_sizes = jnp.arange(LEVELS - 1, dtype=jnp.int32) % 4 + 1
    shuffled = jax.random.permutation(key, step_sizes)
    return jnp.concatenate([jnp.zeros((1,), jnp.int32), jnp.cumsum(shuffled).astype(jnp.int32)])


def touch_ends(array, rng, low, top_value):
    place = [jax.random.randint(jax.random.fold_in(rng, axis), (), 0, length) for axis, length in enumerate(array.shape)]
    main_axis = array.shape.index(max(array.shape))
    next_to = place[:main_axis] + [(place[main_axis] + 1) % array.shape[main_axis]] + place[main_axis + 1:]
    return array.at[tuple(place)].set(low).at[tuple(next_to)].set(top_value)


def steps_of(rng, dims, shards, low, high):
    def one(axis_at, blocks):
        steps = jax.random.uniform(jax.random.fold_in(jax.random.fold_in(rng, 6), axis_at), (blocks,), jnp.float32, low / len(shards), high / len(shards))
        return jnp.repeat(jnp.exp(steps), dims[axis_at] // blocks).reshape((-1,) + (1,) * (len(dims) - axis_at - 1))

    gain = one(*shards[0])
    for cut in shards[1:]:
        gain = gain * one(*cut)
    return gain


def setup_inputs(seed: int = 0) -> dict:
    streams_of = jax.random.split(jax.random.key(seed), 6)
    return {
        "gradient": draw_gradient(jax.random.fold_in(streams_of[5], 71), 0),
        "thresholds": touch_ends(jax.random.randint(streams_of[1], (REPLICAS, ROWS, D), 0, 4096), jax.random.fold_in(streams_of[1], 1), 0, 4095).astype(jnp.int32),
        "sign_bits": touch_ends((jax.random.randint(streams_of[2], (D,), 0, 2) < 1).astype(jnp.int32), jax.random.fold_in(streams_of[2], 1), 0, 1),
        "levels": draw_levels(jax.random.fold_in(streams_of[5], 71), 0),
        "clip_rms": jnp.clip(jax.random.uniform(streams_of[4], (1,), jnp.float32, 0.5, 1.0), 0.5, 1.0),
    }


epsilon = 1e-06
sharpness = 16.0
dither_range = 4096.0

def hadamard_matrix(size):
    position = jnp.arange(size, dtype=jnp.int32)
    parity = jnp.zeros((size, size), jnp.int32)
    for bit_index in range(size.bit_length() - 1):
        parity = parity + (position[:, None] >> bit_index & 1) * (position[None, :] >> bit_index & 1)
    return (1 - 2 * (parity % 2)).astype(jnp.float32)

def rotate_rows(rows, sign_flip, hadamard):
    signed = rows * sign_flip.astype(jnp.bfloat16)
    blocks = signed.reshape(-1, hadamard.shape[0])
    product = jnp.dot(blocks, hadamard.astype(jnp.bfloat16), preferred_element_type=jnp.float32)
    return product * (1.0 / math.sqrt(hadamard.shape[0]))

def encode_units(normed, dither, table, units):
    low_level = jnp.zeros_like(normed) + table[0]
    high_level = jnp.zeros_like(normed) + table[1]
    low_unit = jnp.zeros_like(normed) + units[0]
    high_unit = jnp.zeros_like(normed) + units[1]
    for position in range(1, table.shape[0] - 1):
        above = normed >= table[position]
        low_level = jnp.where(above, table[position], low_level)
        high_level = jnp.where(above, table[position + 1], high_level)
        low_unit = jnp.where(above, units[position], low_unit)
        high_unit = jnp.where(above, units[position + 1], high_unit)
    fraction = (normed - low_level) / (high_level - low_level)
    bottom = jax.nn.sigmoid(-sharpness * dither)
    upper_end = jax.nn.sigmoid(sharpness * (1.0 - dither))
    ramp = (jax.nn.sigmoid(sharpness * (fraction - dither)) - bottom) / (upper_end - bottom)
    return low_unit + (high_unit - low_unit) * ramp

def restore_blocks(code_sum, block_scale, hadamard, top_unit, count):
    merged = (2.0 * code_sum / top_unit - count) * block_scale[:, None]
    product = jnp.dot(merged, hadamard, precision=lax.Precision.HIGHEST)
    return product * (1.0 / math.sqrt(hadamard.shape[0]))

def reference(gradient, thresholds, sign_bits, levels, clip_rms):
    hadamard = hadamard_matrix(BLOCK)
    sign_flip = (1 - 2 * sign_bits).astype(jnp.float32)
    units = levels.astype(jnp.float32)
    top_unit = units[LEVELS - 1]
    table = 2.0 * units / top_unit - 1.0
    block_count = D // BLOCK

    def largest(carry, rows):
        rotated = rotate_rows(rows, sign_flip, hadamard)
        return (jnp.maximum(carry, lax.optimization_barrier(jnp.max(jnp.abs(rotated), axis=1))), None)
    peaks, _ = lax.scan(largest, jnp.zeros((ROWS * block_count,), jnp.float32), gradient)
    block_scale = peaks + epsilon

    def accumulate(carry, inputs):
        rows, draws = inputs
        rotated = rotate_rows(rows, sign_flip, hadamard)
        normed = rotated / block_scale[:, None]
        dither = (draws.reshape(-1, BLOCK).astype(jnp.float32) + 0.5) / dither_range
        return (carry + encode_units(normed, dither, table, units), None)
    code_sum, _ = lax.scan(accumulate, jnp.zeros((ROWS * block_count, BLOCK), jnp.float32), (gradient, thresholds))
    restored = restore_blocks(code_sum, block_scale, hadamard, top_unit, float(REPLICAS))
    restored = (restored.reshape(ROWS, block_count, BLOCK) * sign_flip.reshape(block_count, BLOCK)[None]).reshape(ROWS, D)
    root_mean = jnp.sqrt(jnp.sum(restored * restored) / (ROWS * D) + epsilon)
    factor = clip_rms[0] / jnp.maximum(root_mean, clip_rms[0])
    return (restored * factor).astype(jnp.bfloat16)
```

```python
import functools
import math

import jax
import jax.numpy as jnp
from jax import lax
from jax.experimental import pallas as pl
from jax.experimental.pallas import tpu as pltpu
from jax.sharding import PartitionSpec as P

BLOCK = 128
MESH = pl.DeviceIdType.MESH
CHUNK = 2
epsilon = 1e-06
sharpness = 16.0
dither_range = 4096.0
LOG2E = math.log2(math.e)


def hadamard_matrix(size):
    position = jnp.arange(size, dtype=jnp.int32)
    parity = jnp.zeros((size, size), jnp.int32)
    for bit_index in range(size.bit_length() - 1):
        parity = parity + (position[:, None] >> bit_index & 1) * (
            position[None, :] >> bit_index & 1
        )
    return (1 - 2 * (parity % 2)).astype(jnp.float32)


def kernel(
    entries, grad, thr, flip, had, levels, clip, out,
    rot, amp, peak, peak_a, peak_b, send, recv_a, part, recv_b, merged, ssq, ssq_in,
    pk_send, pk_a, pk_b, a_send, a_recv, b_send, b_recv, q_send, q_recv, g_send, z_recv, p_recv,
):
    me, core = lax.axis_index("dp"), lax.axis_index("tensor")
    x, y, z = me % 2, (me // 2) % 2, me // 4
    blocks = rot.shape[0]
    half = blocks // 2
    chunks = half // CHUNK
    count = 16.0
    inv_root = 1.0 / math.sqrt(BLOCK)

    def plane_peer(d):
        dx, dy = d % 2, d // 2
        return ((y + dy) % 2) * 2 + (x + dx) % 2

    def z_peer(d):
        return (z + d) % 4

    def dev(zz, q, cc=None):
        return (zz * 4 + q, core if cc is None else cc)

    def remote(src, dst, ss, rs, where):
        return pltpu.make_async_remote_copy(
            src_ref=src, dst_ref=dst, send_sem=ss, recv_sem=rs, device_id=where, device_id_type=MESH
        )

    mine = y * 2 + x
    others = [(d, c) for d in range(16) for c in range(2) if (d, c) != (0, 0)]

    barrier = pltpu.get_barrier_semaphore()
    for d, c in others:
        pl.semaphore_signal(
            barrier, inc=1, device_id=((me + d) % 16, (core + c) % 2), device_id_type=MESH
        )

    hb = had[...].astype(jnp.bfloat16)
    peak[...] = jnp.zeros_like(peak)

    def rotate(b, _):
        cols = pl.ds(pl.multiple_of(b * BLOCK, BLOCK), BLOCK)
        signed = grad[:, cols] * flip[pl.ds(b, 1), :].astype(jnp.bfloat16)
        rot[b] = jnp.dot(signed, hb, preferred_element_type=jnp.float32)
        turned = lax.dot_general(
            hb, signed, (((0,), (1,)), ((), ())), preferred_element_type=jnp.float32
        )
        peak[pl.ds(b, 1), :] = jnp.max(jnp.abs(turned), axis=0, keepdims=True) * inv_root
        return 0

    lax.fori_loop(0, blocks, rotate, 0)

    def amplitude(b, _):
        cols = pl.ds(pl.multiple_of(b * BLOCK, BLOCK), BLOCK)
        power = (thr[:, cols].astype(jnp.float32) + 0.5) * (sharpness * LOG2E / dither_range)
        amp[b] = jnp.exp2(power)
        return 0

    pl.semaphore_wait(barrier, len(others))

    copies = []
    first = [
        remote(peak, peak_a.at[d - 1], pk_send.at[d - 1], pk_a.at[d - 1], dev(z, plane_peer(d)))
        for d in range(1, 4)
    ]
    for c in first:
        c.start()
    lax.fori_loop(0, half, amplitude, 0)
    for c in first:
        c.wait()
    peak[...] = jnp.maximum(
        jnp.maximum(peak[...], peak_a[0]), jnp.maximum(peak_a[1], peak_a[2])
    )
    second = [
        remote(peak, peak_b.at[d - 1], pk_send.at[d + 2], pk_b.at[d - 1], dev(z_peer(d), mine))
        for d in range(1, 4)
    ]
    for c in second:
        c.start()
    lax.fori_loop(half, blocks, amplitude, 0)
    for c in second:
        c.wait()
    scale = (
        jnp.maximum(jnp.maximum(peak[...], peak_b[0]), jnp.maximum(peak_b[1], peak_b[2])) + epsilon
    )
    units = [levels[p].astype(jnp.float32) for p in range(16)]
    top = units[15]
    packed = [units[p] + (units[p + 1] - units[p]) * 0.125 for p in range(15)]
    half_top = 0.5 * top
    peak_a[0] = scale
    peak_a[1] = (half_top * inv_root) / scale

    lane = lax.broadcasted_iota(jnp.int32, (BLOCK, BLOCK), 1)
    row = lax.broadcasted_iota(jnp.int32, (BLOCK, BLOCK), 0)
    decay = math.exp(-sharpness)

    def code_of(b):
        inverse = jnp.sum(
            jnp.where(lane == row, peak_a[1, pl.ds(b, 1), :], 0.0), axis=1, keepdims=True
        )
        place = rot[b] * inverse + half_top
        pack = jnp.zeros_like(place) + packed[0]
        for p in range(1, 15):
            pack = jnp.where(place >= units[p], packed[p], pack)
        low = jnp.floor(pack)
        gap = (pack - low) * 8.0
        inv_gap = ((10.0 - gap) * gap - 35.0) * gap + 50.0
        w = jnp.exp2((place - low) * inv_gap * (-sharpness * LOG2E / 24.0))
        a = amp[b]
        upper = (1.0 - w) * (a * (decay / (1.0 - decay)) + 1.0 / (1.0 - decay))
        return low + gap * (upper / (1.0 + a * w))

    def plane_copy(c, d):
        return remote(
            send.at[c, plane_peer(d)], recv_a.at[c, d - 1], a_send.at[c, d - 1],
            a_recv.at[c, d - 1], dev(z, plane_peer(d)),
        )

    def z_copy(c, d):
        return remote(
            part.at[c, z_peer(d)], recv_b.at[c, d - 1], b_send.at[c, d - 1],
            b_recv.at[c, d - 1], dev(z_peer(d), mine),
        )

    def encode_chunk(c):
        for h in range(2):
            def one(k, _):
                code = code_of(h * half + c * CHUNK + k)
                for zz in range(4):
                    for yy in range(2):
                        at = 16 * (2 * zz + yy)
                        send[c, yy * 2 + h, zz, k] = code[at:at + 16]
                return 0
            lax.fori_loop(0, CHUNK, one, 0)
        for d in range(1, 4):
            plane_copy(c, d).start()

    def add_plane(c):
        for d in range(1, 4):
            plane_copy(c, d).wait_recv()
        part[c] = (send[c, mine] + recv_a[c, 0]) + (recv_a[c, 1] + recv_a[c, 2])
        for d in range(1, 4):
            z_copy(c, d).start()

    for c in range(chunks):
        encode_chunk(c)
        if c >= 2:
            add_plane(c - 2)
    for c in range(max(chunks - 2, 0), chunks):
        add_plane(c)

    group = 2 * z + y
    lane16 = lax.broadcasted_iota(jnp.int32, (16, BLOCK), 1)
    row16 = lax.broadcasted_iota(jnp.int32, (16, BLOCK), 0)
    own_rows = lane16 == row16 + 16 * group
    total = jnp.zeros((16, BLOCK), jnp.float32)
    for c in range(chunks):
        for d in range(1, 4):
            z_copy(c, d).wait_recv()
        sums = (part[c, z] + recv_b[c, 0]) + (recv_b[c, 1] + recv_b[c, 2])
        for k in range(CHUNK):
            b = x * half + c * CHUNK + k
            own_scale = jnp.sum(
                jnp.where(own_rows, peak_a[0, pl.ds(b, 1), :], 0.0), axis=1, keepdims=True
            )
            value = (2.0 * sums[k] / top - count) * own_scale
            merged[c * CHUNK + k] = value
            total = total + value * value
    ssq[...] = total[0:8] + total[8:16]

    ssq_copies = [
        remote(
            ssq, ssq_in.at[i], q_send.at[i], q_recv.at[i], ((me + d) % 16, (core + c) % 2)
        )
        for i, (d, c) in enumerate(others)
    ]
    for c in ssq_copies:
        c.start()

    flat = merged[...].reshape(half * 16, BLOCK)
    hi = flat.astype(jnp.bfloat16)
    rest = flat - hi.astype(jnp.float32)
    mid = rest.astype(jnp.bfloat16)
    lo = (rest - mid.astype(jnp.float32)).astype(jnp.bfloat16)
    restored = (
        jnp.dot(hi, hb, preferred_element_type=jnp.float32)
        + jnp.dot(mid, hb, preferred_element_type=jnp.float32)
        + jnp.dot(lo, hb, preferred_element_type=jnp.float32)
    ) * inv_root
    merged[...] = restored.reshape(half, 16, BLOCK)

    for c in ssq_copies:
        c.wait_recv()
    squares = jnp.sum(ssq[...] + jnp.sum(ssq_in[...], axis=0), keepdims=True)
    root_mean = jnp.sqrt(squares / entries + epsilon)
    factor = clip[0] / jnp.maximum(root_mean, clip[0])

    def piece(zz, yy, xx):
        return out.at[
            pl.ds(pl.multiple_of(16 * (2 * zz + yy), 16), 16),
            pl.ds(pl.multiple_of(xx * (half * BLOCK), BLOCK), half * BLOCK),
        ]

    for k in range(half):
        b = x * half + k
        out[
            pl.ds(pl.multiple_of(16 * group, 16), 16),
            pl.ds(pl.multiple_of(b * BLOCK, BLOCK), BLOCK),
        ] = (merged[k] * flip[pl.ds(b, 1), :] * factor).astype(jnp.bfloat16)

    own = piece(z, y, x)
    sent = []

    def go(copy):
        copy.start()
        sent.append(copy)

    for d in range(1, 4):
        go(remote(own, own, g_send.at[d - 1, 0], z_recv.at[d - 1], dev(z_peer(d), mine)))
    for s in range(4):
        zs = (z + 4 - s) % 4
        here = piece(zs, y, x)
        if s:
            remote(here, here, g_send.at[s - 1, 0], z_recv.at[s - 1], dev(z, mine)).wait_recv()
        for d in range(1, 4):
            go(remote(here, here, g_send.at[s, d], p_recv.at[s, d - 1], dev(z, plane_peer(d))))
    for s in range(4):
        zs = (z + 4 - s) % 4
        for d in range(1, 4):
            dx, dy = d % 2, d // 2
            there = piece(zs, (y + dy) % 2, (x + dx) % 2)
            remote(there, there, g_send.at[s, d], p_recv.at[s, d - 1], dev(z, plane_peer(d))).wait_recv()

    for c in range(chunks):
        for d in range(1, 4):
            plane_copy(c, d).wait_send()
            z_copy(c, d).wait_send()
    for c in ssq_copies:
        c.wait_send()
    for c in sent:
        c.wait_send()


def fused_body(gradient, thresholds, sign_bits, levels, clip_rms):
    rows, columns = gradient.shape[1], gradient.shape[2]
    blocks = columns // BLOCK
    half = blocks // 2
    chunks = half // CHUNK
    flip = (1 - 2 * sign_bits).astype(jnp.float32).reshape(blocks, BLOCK)
    entries = float(rows * lax.axis_size("tensor") * columns)
    vmem = pl.BlockSpec(memory_space=pltpu.VMEM)
    smem = pl.BlockSpec(memory_space=pltpu.SMEM)
    f32 = jnp.float32
    padded = -(-blocks // 8) * 8
    dma = pltpu.SemaphoreType.DMA
    return pl.pallas_call(
        functools.partial(kernel, entries),
        out_shape=jax.ShapeDtypeStruct((rows, columns), jnp.bfloat16),
        in_specs=[vmem, vmem, vmem, vmem, smem, smem],
        out_specs=vmem,
        scratch_shapes=[
            pltpu.VMEM((blocks, rows, BLOCK), f32),
            pltpu.VMEM((blocks, rows, BLOCK), f32),
            pltpu.VMEM((padded, BLOCK), f32),
            pltpu.VMEM((3, padded, BLOCK), f32),
            pltpu.VMEM((3, padded, BLOCK), f32),
            pltpu.VMEM((chunks, 4, 4, CHUNK, 16, BLOCK), f32),
            pltpu.VMEM((chunks, 3, 4, CHUNK, 16, BLOCK), f32),
            pltpu.VMEM((chunks, 4, CHUNK, 16, BLOCK), f32),
            pltpu.VMEM((chunks, 3, CHUNK, 16, BLOCK), f32),
            pltpu.VMEM((half, 16, BLOCK), f32),
            pltpu.VMEM((8, BLOCK), f32),
            pltpu.VMEM((31, 8, BLOCK), f32),
            dma((6,)), dma((3,)), dma((3,)),
            dma((chunks, 3)), dma((chunks, 3)), dma((chunks, 3)), dma((chunks, 3)),
            dma((31,)), dma((31,)),
            dma((4, 4)), dma((3,)), dma((4, 3)),
        ],
        compiler_params=pltpu.CompilerParams(
            collective_id=0, has_side_effects=True, vmem_limit_bytes=40 * 1024 * 1024
        ),
    )(gradient[0], thresholds[0], flip, hadamard_matrix(BLOCK), levels, clip_rms)


def encode_units(normed, dither, table, units):
    low_level = jnp.zeros_like(normed) + table[0]
    high_level = jnp.zeros_like(normed) + table[1]
    low_unit = jnp.zeros_like(normed) + units[0]
    high_unit = jnp.zeros_like(normed) + units[1]
    for position in range(1, table.shape[0] - 1):
        above = normed >= table[position]
        low_level = jnp.where(above, table[position], low_level)
        high_level = jnp.where(above, table[position + 1], high_level)
        low_unit = jnp.where(above, units[position], low_unit)
        high_unit = jnp.where(above, units[position + 1], high_unit)
    fraction = (normed - low_level) / (high_level - low_level)
    bottom = jax.nn.sigmoid(-sharpness * dither)
    upper_end = jax.nn.sigmoid(sharpness * (1.0 - dither))
    ramp = (jax.nn.sigmoid(sharpness * (fraction - dither)) - bottom) / (upper_end - bottom)
    return low_unit + (high_unit - low_unit) * ramp


def restore_blocks(code_sum, block_scale, hadamard, top_unit, count):
    merged = (2.0 * code_sum / top_unit - count) * block_scale[:, None]
    product = jnp.dot(merged, hadamard, precision=lax.Precision.HIGHEST)
    return product * (1.0 / math.sqrt(hadamard.shape[0]))


def body(gradient, thresholds, sign_bits, levels, clip_rms):
    row_count = gradient.shape[1]
    columns = gradient.shape[2]
    block_count = columns // BLOCK
    replica_count = float(lax.axis_size("dp"))
    hadamard = hadamard_matrix(BLOCK)
    sign_flip = (1 - 2 * sign_bits).astype(jnp.float32)
    units = levels.astype(jnp.float32)
    top_unit = units[levels.shape[0] - 1]
    table = 2.0 * units / top_unit - 1.0
    signed = gradient[0] * sign_flip.astype(jnp.bfloat16)
    blocks = signed.reshape(row_count * block_count, BLOCK)
    rotated = jnp.dot(blocks, hadamard.astype(jnp.bfloat16), preferred_element_type=jnp.float32) * (
        1.0 / math.sqrt(BLOCK)
    )
    local_peak = jnp.max(jnp.abs(rotated), axis=1)
    block_scale = lax.pmax(local_peak, "dp") + epsilon
    normed = rotated / block_scale[:, None]
    dither = (
        thresholds[0].reshape(row_count * block_count, BLOCK).astype(jnp.float32) + 0.5
    ) / dither_range
    code_values = encode_units(normed, dither, table, units)
    flip_blocks = sign_flip.reshape(block_count, BLOCK)
    entries = float(row_count * lax.axis_size("tensor") * columns)
    owned_rows = row_count * block_count // lax.axis_size("dp")
    first_row = lax.axis_index("dp") * owned_rows
    owned_sum = lax.psum_scatter(code_values, "dp", scatter_dimension=0, tiled=True)
    owned_scale = lax.dynamic_slice_in_dim(block_scale, first_row, owned_rows, 0)
    block_ids = (first_row + jnp.arange(owned_rows, dtype=jnp.int32)) % block_count
    one_hot = (block_ids[:, None] == jnp.arange(block_count, dtype=jnp.int32)[None, :]).astype(
        jnp.bfloat16
    )
    owned_flip = jnp.dot(
        one_hot, flip_blocks.astype(jnp.bfloat16), preferred_element_type=jnp.float32
    )
    restored = (
        restore_blocks(owned_sum, owned_scale, hadamard, top_unit, replica_count) * owned_flip
    )
    squares = lax.psum(jnp.sum(restored * restored), ("dp", "tensor"))
    root_mean = jnp.sqrt(squares / entries + epsilon)
    factor = clip_rms[0] / jnp.maximum(root_mean, clip_rms[0])
    owned_part = (restored * factor).astype(jnp.bfloat16)
    gathered = lax.all_gather(owned_part, "dp", axis=0, tiled=True)
    return gathered.reshape(row_count, columns)


def solution(mesh):
    in_specs = (P("dp", "tensor", None), P("dp", "tensor", None), P(), P(), P())
    out_specs = P("tensor", None)
    sixteen = mesh.shape["dp"] == 16 and mesh.shape["tensor"] == 2
    call = fused_body if sixteen else body
    return jax.shard_map(call, mesh=mesh, in_specs=in_specs, out_specs=out_specs, check_vma=False)
```

```python
import functools
import math

import jax
import jax.numpy as jnp
from jax import lax
from jax.experimental import pallas as pl
from jax.experimental.pallas import tpu as pltpu
from jax.sharding import PartitionSpec as P

BLOCK = 128
MESH = pl.DeviceIdType.MESH
LOADS = 4
GUARD = 64
CHUNK = 2
epsilon = 1e-06
sharpness = 16.0
dither_range = 4096.0
LOG2E = math.log2(math.e)


def hadamard_matrix(size):
    position = jnp.arange(size, dtype=jnp.int32)
    parity = jnp.zeros((size, size), jnp.int32)
    for bit_index in range(size.bit_length() - 1):
        parity = parity + (position[:, None] >> bit_index & 1) * (
            position[None, :] >> bit_index & 1
        )
    return (1 - 2 * (parity % 2)).astype(jnp.float32)


def kernel(
    entries, grad_in, thr_in, sign_in, levels, clip, out,
    grad, thr, sign, flip, load,
    rot, amp, peak, peak_a, peak_b, send, recv_a, part, recv_b, merged, ssq, ssq_in,
    pk_send, pk_a, pk_b, a_send, a_recv, b_send, b_recv, q_send, q_recv, g_send, z_recv, p_recv,
):
    me, core = lax.axis_index("dp"), lax.axis_index("tensor")
    x, y, z = me % 2, (me // 2) % 2, me // 4
    blocks = rot.shape[0]
    half = blocks // 2
    chunks = half // CHUNK
    count = 16.0
    inv_root = 1.0 / math.sqrt(BLOCK)

    def plane_peer(d):
        dx, dy = d % 2, d // 2
        return ((y + dy) % 2) * 2 + (x + dx) % 2

    def z_peer(d):
        return (z + d) % 4

    def dev(zz, q, cc=None):
        return (zz * 4 + q, core if cc is None else cc)

    def remote(src, dst, ss, rs, where):
        return pltpu.make_async_remote_copy(
            src_ref=src, dst_ref=dst, send_sem=ss, recv_sem=rs, device_id=where, device_id_type=MESH
        )

    mine = y * 2 + x
    others = [(d, c) for d in range(16) for c in range(2) if (d, c) != (0, 0)]

    fetch_sign = pltpu.make_async_copy(sign_in, sign, load.at[0])
    fetch_sign.start()
    quarter = grad.shape[1] // LOADS
    fetch_grad = [
        pltpu.make_async_copy(
            grad_in.at[0, :, pl.ds(i * quarter, quarter)],
            grad.at[:, pl.ds(i * quarter, quarter)],
            load.at[i + 2],
        )
        for i in range(LOADS)
    ]
    for c in fetch_grad:
        c.start()
    fetch_thr = pltpu.make_async_copy(thr_in.at[0], thr, load.at[1])
    fetch_thr.start()

    barrier = pltpu.get_barrier_semaphore()
    for d, c in others:
        pl.semaphore_signal(
            barrier, inc=1, device_id=((me + d) % 16, (core + c) % 2), device_id_type=MESH
        )

    lane = lax.broadcasted_iota(jnp.int32, (BLOCK, BLOCK), 1)
    row = lax.broadcasted_iota(jnp.int32, (BLOCK, BLOCK), 0)
    bits = lane & row
    bits = bits ^ (bits >> 4)
    bits = bits ^ (bits >> 2)
    bits = bits ^ (bits >> 1)
    hb = (1 - 2 * (bits & 1)).astype(jnp.float32).astype(jnp.bfloat16)
    fetch_sign.wait()
    flip[...] = (1 - 2 * sign[...]).astype(jnp.float32)
    peak[...] = jnp.zeros_like(peak)

    def rotate(b, _):
        cols = pl.ds(pl.multiple_of(b * BLOCK, BLOCK), BLOCK)
        signed = grad[:, cols] * flip[pl.ds(b, 1), :].astype(jnp.bfloat16)
        rot[b] = jnp.dot(signed, hb, preferred_element_type=jnp.float32)
        turned = lax.dot_general(
            hb, signed, (((0,), (1,)), ((), ())), preferred_element_type=jnp.float32
        )
        peak[pl.ds(b, 1), :] = jnp.max(jnp.abs(turned), axis=0, keepdims=True) * inv_root
        return 0

    for i in range(LOADS):
        fetch_grad[i].wait()
        lax.fori_loop(i * blocks // LOADS, (i + 1) * blocks // LOADS, rotate, 0)

    def amplitude(b, _):
        cols = pl.ds(pl.multiple_of(b * BLOCK, BLOCK), BLOCK)
        power = (thr[:, cols].astype(jnp.float32) + 0.5) * (sharpness * LOG2E / dither_range)
        amp[b] = jnp.exp2(power)
        return 0

    pl.semaphore_wait(barrier, len(others))

    copies = []
    first = [
        remote(peak, peak_a.at[d - 1], pk_send.at[d - 1], pk_a.at[d - 1], dev(z, plane_peer(d)))
        for d in range(1, 4)
    ]
    for c in first:
        c.start()
    fetch_thr.wait()
    lax.fori_loop(0, half, amplitude, 0)
    for c in first:
        c.wait()
    peak[...] = jnp.maximum(
        jnp.maximum(peak[...], peak_a[0]), jnp.maximum(peak_a[1], peak_a[2])
    )
    second = [
        remote(peak, peak_b.at[d - 1], pk_send.at[d + 2], pk_b.at[d - 1], dev(z_peer(d), mine))
        for d in range(1, 4)
    ]
    for c in second:
        c.start()
    lax.fori_loop(half, blocks, amplitude, 0)
    for c in second:
        c.wait()
    scale = (
        jnp.maximum(jnp.maximum(peak[...], peak_b[0]), jnp.maximum(peak_b[1], peak_b[2])) + epsilon
    )
    units = [levels[p].astype(jnp.float32) for p in range(16)]
    top = units[15]
    packed = [units[p] + (units[p + 1] - units[p]) * 0.125 for p in range(15)]
    half_top = 0.5 * top
    peak_a[0] = scale
    peak_a[1] = (half_top * inv_root) / scale

    decay = math.exp(-sharpness)
    step = (2.0**20 - 2.0 * GUARD) / top
    shift = 2.0 * GUARD * count / (2.0**20 - 2.0 * GUARD) + count

    def code_of(b):
        inverse = jnp.sum(
            jnp.where(lane == row, peak_a[1, pl.ds(b, 1), :], 0.0), axis=1, keepdims=True
        )
        place = rot[b] * inverse + half_top
        pack = jnp.zeros_like(place) + packed[0]
        for p in range(1, 15):
            pack = jnp.where(place >= units[p], packed[p], pack)
        low = jnp.floor(pack)
        gap = (pack - low) * 8.0
        inv_gap = ((10.0 - gap) * gap - 35.0) * gap + 50.0
        w = jnp.exp2((place - low) * inv_gap * (-sharpness * LOG2E / 24.0))
        a = amp[b]
        upper = (1.0 - w) * (a * (decay / (1.0 - decay)) + 1.0 / (1.0 - decay))
        return low + gap * (upper / (1.0 + a * w))

    def plane_copy(c, d):
        return remote(
            send.at[c, plane_peer(d)], recv_a.at[c, d - 1], a_send.at[c, d - 1],
            a_recv.at[c, d - 1], dev(z, plane_peer(d)),
        )

    def z_copy(c, d):
        return remote(
            part.at[c, z_peer(d)], recv_b.at[c, d - 1], b_send.at[c, d - 1],
            b_recv.at[c, d - 1], dev(z_peer(d), mine),
        )

    def encode_chunk(c):
        for h in range(2):
            def one(k, _):
                number = (code_of(h * half + c * CHUNK + k) * step + (GUARD + 0.5)).astype(jnp.int32)
                number = jnp.clip(number, 0, 2**20 - 1)
                high = ((number >> 4) - 2**15).astype(jnp.int16)
                nibble = number & 15
                for yy in range(2):
                    four = jnp.full((16, BLOCK), -(2**15), jnp.int32)
                    for zz in range(4):
                        at = 16 * (2 * zz + yy)
                        send[c, yy * 2 + h, zz, k] = high[at:at + 16]
                        four = four + (nibble[at:at + 16] << (4 * zz))
                    send[c, yy * 2 + h, 4, k] = four.astype(jnp.int16)
                return 0
            lax.fori_loop(0, CHUNK, one, 0)
        for d in range(1, 4):
            plane_copy(c, d).start()

    def add_plane(c):
        for d in range(1, 4):
            plane_copy(c, d).wait_recv()
        sources = [send.at[c, mine], recv_a.at[c, 0], recv_a.at[c, 1], recv_a.at[c, 2]]
        fours = [ref[4].astype(jnp.int32) + 2**15 for ref in sources]
        for zz in range(4):
            upper = sum(ref[zz].astype(jnp.int32) for ref in sources) + 4 * 2**15
            lower = sum((four >> (4 * zz)) & 15 for four in fours)
            part[c, zz] = (upper * 16 + lower).astype(jnp.float32)
        for d in range(1, 4):
            z_copy(c, d).start()

    for c in range(chunks):
        encode_chunk(c)
        if c >= 2:
            add_plane(c - 2)
    for c in range(max(chunks - 2, 0), chunks):
        add_plane(c)

    group = 2 * z + y
    lane16 = lax.broadcasted_iota(jnp.int32, (16, BLOCK), 1)
    row16 = lax.broadcasted_iota(jnp.int32, (16, BLOCK), 0)
    own_rows = lane16 == row16 + 16 * group
    total = jnp.zeros((16, BLOCK), jnp.float32)
    for c in range(chunks):
        for d in range(1, 4):
            z_copy(c, d).wait_recv()
        sums = (part[c, z] + recv_b[c, 0]) + (recv_b[c, 1] + recv_b[c, 2])
        for k in range(CHUNK):
            b = x * half + c * CHUNK + k
            own_scale = jnp.sum(
                jnp.where(own_rows, peak_a[0, pl.ds(b, 1), :], 0.0), axis=1, keepdims=True
            )
            value = (sums[k] * (2.0 / (step * top)) - shift) * own_scale
            merged[c * CHUNK + k] = value
            total = total + value * value
    ssq[...] = total[0:8] + total[8:16]

    ssq_copies = [
        remote(
            ssq, ssq_in.at[i], q_send.at[i], q_recv.at[i], ((me + d) % 16, (core + c) % 2)
        )
        for i, (d, c) in enumerate(others)
    ]
    for c in ssq_copies:
        c.start()

    flat = merged[...].reshape(half * 16, BLOCK)
    hi = flat.astype(jnp.bfloat16)
    rest = flat - hi.astype(jnp.float32)
    mid = rest.astype(jnp.bfloat16)
    lo = (rest - mid.astype(jnp.float32)).astype(jnp.bfloat16)
    restored = (
        jnp.dot(hi, hb, preferred_element_type=jnp.float32)
        + jnp.dot(mid, hb, preferred_element_type=jnp.float32)
        + jnp.dot(lo, hb, preferred_element_type=jnp.float32)
    ) * inv_root
    merged[...] = restored.reshape(half, 16, BLOCK)

    for c in ssq_copies:
        c.wait_recv()
    squares = jnp.sum(ssq[...] + jnp.sum(ssq_in[...], axis=0), keepdims=True)
    root_mean = jnp.sqrt(squares / entries + epsilon)
    factor = clip[0] / jnp.maximum(root_mean, clip[0])

    def piece(zz, yy, xx):
        return out.at[
            pl.ds(pl.multiple_of(16 * (2 * zz + yy), 16), 16),
            pl.ds(pl.multiple_of(xx * (half * BLOCK), BLOCK), half * BLOCK),
        ]

    for k in range(half):
        b = x * half + k
        out[
            pl.ds(pl.multiple_of(16 * group, 16), 16),
            pl.ds(pl.multiple_of(b * BLOCK, BLOCK), BLOCK),
        ] = (merged[k] * flip[pl.ds(b, 1), :] * factor).astype(jnp.bfloat16)

    own = piece(z, y, x)
    sent = []

    def go(copy):
        copy.start()
        sent.append(copy)

    for d in range(1, 4):
        go(remote(own, own, g_send.at[d - 1, 0], z_recv.at[d - 1], dev(z_peer(d), mine)))
    for s in range(4):
        zs = (z + 4 - s) % 4
        here = piece(zs, y, x)
        if s:
            remote(here, here, g_send.at[s - 1, 0], z_recv.at[s - 1], dev(z, mine)).wait_recv()
        for d in range(1, 4):
            go(remote(here, here, g_send.at[s, d], p_recv.at[s, d - 1], dev(z, plane_peer(d))))
    for s in range(4):
        zs = (z + 4 - s) % 4
        for d in range(1, 4):
            dx, dy = d % 2, d // 2
            there = piece(zs, (y + dy) % 2, (x + dx) % 2)
            remote(there, there, g_send.at[s, d], p_recv.at[s, d - 1], dev(z, plane_peer(d))).wait_recv()

    for c in range(chunks):
        for d in range(1, 4):
            plane_copy(c, d).wait_send()
            z_copy(c, d).wait_send()
    for c in ssq_copies:
        c.wait_send()
    for c in sent:
        c.wait_send()


def fused_body(gradient, thresholds, sign_bits, levels, clip_rms):
    rows, columns = gradient.shape[1], gradient.shape[2]
    blocks = columns // BLOCK
    half = blocks // 2
    chunks = half // CHUNK
    entries = float(rows * lax.axis_size("tensor") * columns)
    vmem = pl.BlockSpec(memory_space=pltpu.VMEM)
    hbm = pl.BlockSpec(memory_space=pl.ANY)
    smem = pl.BlockSpec(memory_space=pltpu.SMEM)
    f32 = jnp.float32
    padded = -(-blocks // 8) * 8
    dma = pltpu.SemaphoreType.DMA
    return pl.pallas_call(
        functools.partial(kernel, entries),
        out_shape=pltpu.VMEM((rows, columns), jnp.bfloat16),
        in_specs=[hbm, hbm, hbm, smem, smem],
        out_specs=vmem,
        scratch_shapes=[
            pltpu.VMEM((rows, columns), jnp.bfloat16),
            pltpu.VMEM((rows, columns), jnp.int32),
            pltpu.VMEM((blocks, BLOCK), jnp.int32),
            pltpu.VMEM((blocks, BLOCK), f32),
            dma((LOADS + 2,)),
            pltpu.VMEM((blocks, rows, BLOCK), f32),
            pltpu.VMEM((blocks, rows, BLOCK), f32),
            pltpu.VMEM((padded, BLOCK), f32),
            pltpu.VMEM((3, padded, BLOCK), f32),
            pltpu.VMEM((3, padded, BLOCK), f32),
            pltpu.VMEM((chunks, 4, 5, CHUNK, 16, BLOCK), jnp.int16),
            pltpu.VMEM((chunks, 3, 5, CHUNK, 16, BLOCK), jnp.int16),
            pltpu.VMEM((chunks, 4, CHUNK, 16, BLOCK), f32),
            pltpu.VMEM((chunks, 3, CHUNK, 16, BLOCK), f32),
            pltpu.VMEM((half, 16, BLOCK), f32),
            pltpu.VMEM((8, BLOCK), f32),
            pltpu.VMEM((31, 8, BLOCK), f32),
            dma((6,)), dma((3,)), dma((3,)),
            dma((chunks, 3)), dma((chunks, 3)), dma((chunks, 3)), dma((chunks, 3)),
            dma((31,)), dma((31,)),
            dma((4, 4)), dma((3,)), dma((4, 3)),
        ],
        compiler_params=pltpu.CompilerParams(
            collective_id=0, has_side_effects=True, vmem_limit_bytes=60 * 1024 * 1024
        ),
    )(gradient, thresholds, sign_bits.reshape(blocks, BLOCK), levels, clip_rms)


def encode_units(normed, dither, table, units):
    low_level = jnp.zeros_like(normed) + table[0]
    high_level = jnp.zeros_like(normed) + table[1]
    low_unit = jnp.zeros_like(normed) + units[0]
    high_unit = jnp.zeros_like(normed) + units[1]
    for position in range(1, table.shape[0] - 1):
        above = normed >= table[position]
        low_level = jnp.where(above, table[position], low_level)
        high_level = jnp.where(above, table[position + 1], high_level)
        low_unit = jnp.where(above, units[position], low_unit)
        high_unit = jnp.where(above, units[position + 1], high_unit)
    fraction = (normed - low_level) / (high_level - low_level)
    bottom = jax.nn.sigmoid(-sharpness * dither)
    upper_end = jax.nn.sigmoid(sharpness * (1.0 - dither))
    ramp = (jax.nn.sigmoid(sharpness * (fraction - dither)) - bottom) / (upper_end - bottom)
    return low_unit + (high_unit - low_unit) * ramp


def restore_blocks(code_sum, block_scale, hadamard, top_unit, count):
    merged = (2.0 * code_sum / top_unit - count) * block_scale[:, None]
    product = jnp.dot(merged, hadamard, precision=lax.Precision.HIGHEST)
    return product * (1.0 / math.sqrt(hadamard.shape[0]))


def body(gradient, thresholds, sign_bits, levels, clip_rms):
    row_count = gradient.shape[1]
    columns = gradient.shape[2]
    block_count = columns // BLOCK
    replica_count = float(lax.axis_size("dp"))
    hadamard = hadamard_matrix(BLOCK)
    sign_flip = (1 - 2 * sign_bits).astype(jnp.float32)
    units = levels.astype(jnp.float32)
    top_unit = units[levels.shape[0] - 1]
    table = 2.0 * units / top_unit - 1.0
    signed = gradient[0] * sign_flip.astype(jnp.bfloat16)
    blocks = signed.reshape(row_count * block_count, BLOCK)
    rotated = jnp.dot(blocks, hadamard.astype(jnp.bfloat16), preferred_element_type=jnp.float32) * (
        1.0 / math.sqrt(BLOCK)
    )
    local_peak = jnp.max(jnp.abs(rotated), axis=1)
    block_scale = lax.pmax(local_peak, "dp") + epsilon
    normed = rotated / block_scale[:, None]
    dither = (
        thresholds[0].reshape(row_count * block_count, BLOCK).astype(jnp.float32) + 0.5
    ) / dither_range
    code_values = encode_units(normed, dither, table, units)
    flip_blocks = sign_flip.reshape(block_count, BLOCK)
    entries = float(row_count * lax.axis_size("tensor") * columns)
    owned_rows = row_count * block_count // lax.axis_size("dp")
    first_row = lax.axis_index("dp") * owned_rows
    owned_sum = lax.psum_scatter(code_values, "dp", scatter_dimension=0, tiled=True)
    owned_scale = lax.dynamic_slice_in_dim(block_scale, first_row, owned_rows, 0)
    block_ids = (first_row + jnp.arange(owned_rows, dtype=jnp.int32)) % block_count
    one_hot = (block_ids[:, None] == jnp.arange(block_count, dtype=jnp.int32)[None, :]).astype(
        jnp.bfloat16
    )
    owned_flip = jnp.dot(
        one_hot, flip_blocks.astype(jnp.bfloat16), preferred_element_type=jnp.float32
    )
    restored = (
        restore_blocks(owned_sum, owned_scale, hadamard, top_unit, replica_count) * owned_flip
    )
    squares = lax.psum(jnp.sum(restored * restored), ("dp", "tensor"))
    root_mean = jnp.sqrt(squares / entries + epsilon)
    factor = clip_rms[0] / jnp.maximum(root_mean, clip_rms[0])
    owned_part = (restored * factor).astype(jnp.bfloat16)
    gathered = lax.all_gather(owned_part, "dp", axis=0, tiled=True)
    return gathered.reshape(row_count, columns)


def solution(mesh):
    in_specs = (P("dp", "tensor", None), P("dp", "tensor", None), P(), P(), P())
    out_specs = P("tensor", None)
    sixteen = mesh.shape["dp"] == 16 and mesh.shape["tensor"] == 2
    call = fused_body if sixteen else body
    return jax.shard_map(call, mesh=mesh, in_specs=in_specs, out_specs=out_specs, check_vma=False)
```

```python
import functools
import math

import jax
import jax.numpy as jnp
from jax import lax
from jax.experimental import pallas as pl
from jax.experimental.pallas import tpu as pltpu
from jax.sharding import PartitionSpec as P

BLOCK = 128
MESH = pl.DeviceIdType.MESH
LOADS = 4
GUARD = 64
CHUNK = 2
epsilon = 1e-06
sharpness = 16.0
dither_range = 4096.0
LOG2E = math.log2(math.e)


def hadamard_matrix(size):
    position = jnp.arange(size, dtype=jnp.int32)
    parity = jnp.zeros((size, size), jnp.int32)
    for bit_index in range(size.bit_length() - 1):
        parity = parity + (position[:, None] >> bit_index & 1) * (
            position[None, :] >> bit_index & 1
        )
    return (1 - 2 * (parity % 2)).astype(jnp.float32)


def kernel(
    entries, grad_in, thr_in, sign_in, levels, clip, out,
    grad, thr, sign, flip, load,
    rot, amp, peak, peak_a, peak_b, send, recv_a, part, recv_b, merged, ssq, ssq_in,
    pk_send, pk_a, pk_b, a_send, a_recv, b_send, b_recv, q_send, q_recv, g_send, z_recv, p_recv,
):
    me, core = lax.axis_index("dp"), lax.axis_index("tensor")
    x, y, z = me % 2, (me // 2) % 2, me // 4
    blocks = rot.shape[0]
    half = blocks // 2
    chunks = half // CHUNK
    count = 16.0
    inv_root = 1.0 / math.sqrt(BLOCK)

    def plane_peer(d):
        dx, dy = d % 2, d // 2
        return ((y + dy) % 2) * 2 + (x + dx) % 2

    def z_peer(d):
        return (z + d) % 4

    def dev(zz, q, cc=None):
        return (zz * 4 + q, core if cc is None else cc)

    def remote(src, dst, ss, rs, where):
        return pltpu.make_async_remote_copy(
            src_ref=src, dst_ref=dst, send_sem=ss, recv_sem=rs, device_id=where, device_id_type=MESH
        )

    mine = y * 2 + x
    others = [(d, c) for d in range(16) for c in range(2) if (d, c) != (0, 0)]

    fetch_sign = pltpu.make_async_copy(sign_in, sign, load.at[0])
    fetch_sign.start()
    quarter = grad.shape[1] // LOADS
    fetch_grad = [
        pltpu.make_async_copy(
            grad_in.at[0, :, pl.ds(i * quarter, quarter)],
            grad.at[:, pl.ds(i * quarter, quarter)],
            load.at[i + 2],
        )
        for i in range(LOADS)
    ]
    for c in fetch_grad:
        c.start()
    fetch_thr = pltpu.make_async_copy(thr_in.at[0], thr, load.at[1])
    fetch_thr.start()

    barrier = pltpu.get_barrier_semaphore()
    for d, c in others:
        pl.semaphore_signal(
            barrier, inc=1, device_id=((me + d) % 16, (core + c) % 2), device_id_type=MESH
        )

    lane = lax.broadcasted_iota(jnp.int32, (BLOCK, BLOCK), 1)
    row = lax.broadcasted_iota(jnp.int32, (BLOCK, BLOCK), 0)
    bits = lane & row
    bits = bits ^ (bits >> 4)
    bits = bits ^ (bits >> 2)
    bits = bits ^ (bits >> 1)
    hb = (1 - 2 * (bits & 1)).astype(jnp.float32).astype(jnp.bfloat16)
    fetch_sign.wait()
    flip[...] = (1 - 2 * sign[...]).astype(jnp.float32)
    peak[...] = jnp.zeros_like(peak)

    def rotate(b, _):
        cols = pl.ds(pl.multiple_of(b * BLOCK, BLOCK), BLOCK)
        signed = grad[:, cols] * flip[pl.ds(b, 1), :].astype(jnp.bfloat16)
        rot[b] = jnp.dot(signed, hb, preferred_element_type=jnp.float32)
        turned = lax.dot_general(
            hb, signed, (((0,), (1,)), ((), ())), preferred_element_type=jnp.float32
        )
        peak[pl.ds(b, 1), :] = jnp.max(jnp.abs(turned), axis=0, keepdims=True) * inv_root
        return 0

    for i in range(LOADS):
        fetch_grad[i].wait()
        lax.fori_loop(i * blocks // LOADS, (i + 1) * blocks // LOADS, rotate, 0, unroll=True)

    def amplitude(b, _):
        cols = pl.ds(pl.multiple_of(b * BLOCK, BLOCK), BLOCK)
        power = (thr[:, cols].astype(jnp.float32) + 0.5) * (sharpness * LOG2E / dither_range)
        amp[b] = jnp.exp2(power)
        return 0

    pl.semaphore_wait(barrier, len(others))

    copies = []
    first = [
        remote(peak, peak_a.at[d - 1], pk_send.at[d - 1], pk_a.at[d - 1], dev(z, plane_peer(d)))
        for d in range(1, 4)
    ]
    for c in first:
        c.start()
    fetch_thr.wait()
    lax.fori_loop(0, half, amplitude, 0, unroll=2)
    for c in first:
        c.wait()
    peak[...] = jnp.maximum(
        jnp.maximum(peak[...], peak_a[0]), jnp.maximum(peak_a[1], peak_a[2])
    )
    second = [
        remote(peak, peak_b.at[d - 1], pk_send.at[d + 2], pk_b.at[d - 1], dev(z_peer(d), mine))
        for d in range(1, 4)
    ]
    for c in second:
        c.start()
    lax.fori_loop(half, blocks, amplitude, 0, unroll=2)
    for c in second:
        c.wait()
    scale = (
        jnp.maximum(jnp.maximum(peak[...], peak_b[0]), jnp.maximum(peak_b[1], peak_b[2])) + epsilon
    )
    units = [levels[p].astype(jnp.float32) for p in range(16)]
    top = units[15]
    packed = [units[p] + (units[p + 1] - units[p]) * 0.125 for p in range(15)]
    half_top = 0.5 * top
    peak_a[0] = scale
    peak_a[1] = (half_top * inv_root) / scale

    decay = math.exp(-sharpness)
    step = (2.0**20 - 2.0 * GUARD) / top
    shift = 2.0 * GUARD * count / (2.0**20 - 2.0 * GUARD) + count

    def code_of(b):
        inverse = jnp.sum(
            jnp.where(lane == row, peak_a[1, pl.ds(b, 1), :], 0.0), axis=1, keepdims=True
        )
        place = rot[b] * inverse + half_top
        pack = jnp.zeros_like(place) + packed[0]
        for p in range(1, 15):
            pack = jnp.where(place >= units[p], packed[p], pack)
        low = jnp.floor(pack)
        gap = (pack - low) * 8.0
        inv_gap = ((10.0 - gap) * gap - 35.0) * gap + 50.0
        w = jnp.exp2((place - low) * inv_gap * (-sharpness * LOG2E / 24.0))
        a = amp[b]
        upper = (1.0 - w) * (a * (decay / (1.0 - decay)) + 1.0 / (1.0 - decay))
        return low + gap * (upper / (1.0 + a * w))

    def plane_copy(c, d):
        return remote(
            send.at[c, plane_peer(d)], recv_a.at[c, d - 1], a_send.at[c, d - 1],
            a_recv.at[c, d - 1], dev(z, plane_peer(d)),
        )

    def z_copy(c, d):
        return remote(
            part.at[c, z_peer(d)], recv_b.at[c, d - 1], b_send.at[c, d - 1],
            b_recv.at[c, d - 1], dev(z_peer(d), mine),
        )

    def encode_chunk(c):
        for h in range(2):
            def one(k, _):
                number = (code_of(h * half + c * CHUNK + k) * step + (GUARD + 0.5)).astype(jnp.int32)
                number = jnp.clip(number, 0, 2**20 - 1)
                high = ((number >> 4) - 2**15).astype(jnp.int16)
                nibble = number & 15
                for yy in range(2):
                    four = jnp.full((16, BLOCK), -(2**15), jnp.int32)
                    for zz in range(4):
                        at = 16 * (2 * zz + yy)
                        send[c, yy * 2 + h, zz, k] = high[at:at + 16]
                        four = four + (nibble[at:at + 16] << (4 * zz))
                    send[c, yy * 2 + h, 4, k] = four.astype(jnp.int16)
                return 0
            lax.fori_loop(0, CHUNK, one, 0, unroll=True)
        for d in range(1, 4):
            plane_copy(c, d).start()

    def add_plane(c):
        for d in range(1, 4):
            plane_copy(c, d).wait_recv()
        sources = [send.at[c, mine], recv_a.at[c, 0], recv_a.at[c, 1], recv_a.at[c, 2]]
        fours = [ref[4].astype(jnp.int32) + 2**15 for ref in sources]
        for zz in range(4):
            upper = sum(ref[zz].astype(jnp.int32) for ref in sources) + 4 * 2**15
            lower = sum((four >> (4 * zz)) & 15 for four in fours)
            part[c, zz] = (upper * 16 + lower).astype(jnp.float32)
        for d in range(1, 4):
            z_copy(c, d).start()

    for c in range(chunks):
        encode_chunk(c)
        if c >= 2:
            add_plane(c - 2)
    for c in range(max(chunks - 2, 0), chunks):
        add_plane(c)

    group = 2 * z + y
    lane16 = lax.broadcasted_iota(jnp.int32, (16, BLOCK), 1)
    row16 = lax.broadcasted_iota(jnp.int32, (16, BLOCK), 0)
    own_rows = lane16 == row16 + 16 * group
    total = jnp.zeros((16, BLOCK), jnp.float32)
    for c in range(chunks):
        for d in range(1, 4):
            z_copy(c, d).wait_recv()
        sums = (part[c, z] + recv_b[c, 0]) + (recv_b[c, 1] + recv_b[c, 2])
        for k in range(CHUNK):
            b = x * half + c * CHUNK + k
            own_scale = jnp.sum(
                jnp.where(own_rows, peak_a[0, pl.ds(b, 1), :], 0.0), axis=1, keepdims=True
            )
            value = (sums[k] * (2.0 / (step * top)) - shift) * own_scale
            merged[c * CHUNK + k] = value
            total = total + value * value
    ssq[...] = total[0:8] + total[8:16]

    ssq_copies = [
        remote(
            ssq, ssq_in.at[i], q_send.at[i], q_recv.at[i], ((me + d) % 16, (core + c) % 2)
        )
        for i, (d, c) in enumerate(others)
    ]
    for c in ssq_copies:
        c.start()

    flat = merged[...].reshape(half * 16, BLOCK)
    hi = flat.astype(jnp.bfloat16)
    rest = flat - hi.astype(jnp.float32)
    mid = rest.astype(jnp.bfloat16)
    lo = (rest - mid.astype(jnp.float32)).astype(jnp.bfloat16)
    restored = (
        jnp.dot(hi, hb, preferred_element_type=jnp.float32)
        + jnp.dot(mid, hb, preferred_element_type=jnp.float32)
        + jnp.dot(lo, hb, preferred_element_type=jnp.float32)
    ) * inv_root
    merged[...] = restored.reshape(half, 16, BLOCK)

    for c in ssq_copies:
        c.wait_recv()
    squares = jnp.sum(ssq[...] + jnp.sum(ssq_in[...], axis=0), keepdims=True)
    root_mean = jnp.sqrt(squares / entries + epsilon)
    factor = clip[0] / jnp.maximum(root_mean, clip[0])

    def piece(zz, yy, xx):
        return out.at[
            pl.ds(pl.multiple_of(16 * (2 * zz + yy), 16), 16),
            pl.ds(pl.multiple_of(xx * (half * BLOCK), BLOCK), half * BLOCK),
        ]

    for k in range(half):
        b = x * half + k
        out[
            pl.ds(pl.multiple_of(16 * group, 16), 16),
            pl.ds(pl.multiple_of(b * BLOCK, BLOCK), BLOCK),
        ] = (merged[k] * flip[pl.ds(b, 1), :] * factor).astype(jnp.bfloat16)

    own = piece(z, y, x)
    sent = []

    def go(copy):
        copy.start()
        sent.append(copy)

    for d in range(1, 4):
        go(remote(own, own, g_send.at[d - 1, 0], z_recv.at[d - 1], dev(z_peer(d), mine)))
    for s in range(4):
        zs = (z + 4 - s) % 4
        here = piece(zs, y, x)
        if s:
            remote(here, here, g_send.at[s - 1, 0], z_recv.at[s - 1], dev(z, mine)).wait_recv()
        for d in range(1, 4):
            go(remote(here, here, g_send.at[s, d], p_recv.at[s, d - 1], dev(z, plane_peer(d))))
    for s in range(4):
        zs = (z + 4 - s) % 4
        for d in range(1, 4):
            dx, dy = d % 2, d // 2
            there = piece(zs, (y + dy) % 2, (x + dx) % 2)
            remote(there, there, g_send.at[s, d], p_recv.at[s, d - 1], dev(z, plane_peer(d))).wait_recv()

    for c in range(chunks):
        for d in range(1, 4):
            plane_copy(c, d).wait_send()
            z_copy(c, d).wait_send()
    for c in ssq_copies:
        c.wait_send()
    for c in sent:
        c.wait_send()


def fused_body(gradient, thresholds, sign_bits, levels, clip_rms):
    rows, columns = gradient.shape[1], gradient.shape[2]
    blocks = columns // BLOCK
    half = blocks // 2
    chunks = half // CHUNK
    entries = float(rows * lax.axis_size("tensor") * columns)
    vmem = pl.BlockSpec(memory_space=pltpu.VMEM)
    hbm = pl.BlockSpec(memory_space=pl.ANY)
    smem = pl.BlockSpec(memory_space=pltpu.SMEM)
    f32 = jnp.float32
    padded = -(-blocks // 8) * 8
    dma = pltpu.SemaphoreType.DMA
    return pl.pallas_call(
        functools.partial(kernel, entries),
        out_shape=pltpu.VMEM((rows, columns), jnp.bfloat16),
        in_specs=[hbm, hbm, hbm, smem, smem],
        out_specs=vmem,
        scratch_shapes=[
            pltpu.VMEM((rows, columns), jnp.bfloat16),
            pltpu.VMEM((rows, columns), jnp.int32),
            pltpu.VMEM((blocks, BLOCK), jnp.int32),
            pltpu.VMEM((blocks, BLOCK), f32),
            dma((LOADS + 2,)),
            pltpu.VMEM((blocks, rows, BLOCK), f32),
            pltpu.VMEM((blocks, rows, BLOCK), f32),
            pltpu.VMEM((padded, BLOCK), f32),
            pltpu.VMEM((3, padded, BLOCK), f32),
            pltpu.VMEM((3, padded, BLOCK), f32),
            pltpu.VMEM((chunks, 4, 5, CHUNK, 16, BLOCK), jnp.int16),
            pltpu.VMEM((chunks, 3, 5, CHUNK, 16, BLOCK), jnp.int16),
            pltpu.VMEM((chunks, 4, CHUNK, 16, BLOCK), f32),
            pltpu.VMEM((chunks, 3, CHUNK, 16, BLOCK), f32),
            pltpu.VMEM((half, 16, BLOCK), f32),
            pltpu.VMEM((8, BLOCK), f32),
            pltpu.VMEM((31, 8, BLOCK), f32),
            dma((6,)), dma((3,)), dma((3,)),
            dma((chunks, 3)), dma((chunks, 3)), dma((chunks, 3)), dma((chunks, 3)),
            dma((31,)), dma((31,)),
            dma((4, 4)), dma((3,)), dma((4, 3)),
        ],
        compiler_params=pltpu.CompilerParams(
            collective_id=0, has_side_effects=True, vmem_limit_bytes=60 * 1024 * 1024
        ),
    )(gradient, thresholds, sign_bits.reshape(blocks, BLOCK), levels, clip_rms)


def encode_units(normed, dither, table, units):
    low_level = jnp.zeros_like(normed) + table[0]
    high_level = jnp.zeros_like(normed) + table[1]
    low_unit = jnp.zeros_like(normed) + units[0]
    high_unit = jnp.zeros_like(normed) + units[1]
    for position in range(1, table.shape[0] - 1):
        above = normed >= table[position]
        low_level = jnp.where(above, table[position], low_level)
        high_level = jnp.where(above, table[position + 1], high_level)
        low_unit = jnp.where(above, units[position], low_unit)
        high_unit = jnp.where(above, units[position + 1], high_unit)
    fraction = (normed - low_level) / (high_level - low_level)
    bottom = jax.nn.sigmoid(-sharpness * dither)
    upper_end = jax.nn.sigmoid(sharpness * (1.0 - dither))
    ramp = (jax.nn.sigmoid(sharpness * (fraction - dither)) - bottom) / (upper_end - bottom)
    return low_unit + (high_unit - low_unit) * ramp


def restore_blocks(code_sum, block_scale, hadamard, top_unit, count):
    merged = (2.0 * code_sum / top_unit - count) * block_scale[:, None]
    product = jnp.dot(merged, hadamard, precision=lax.Precision.HIGHEST)
    return product * (1.0 / math.sqrt(hadamard.shape[0]))


def body(gradient, thresholds, sign_bits, levels, clip_rms):
    row_count = gradient.shape[1]
    columns = gradient.shape[2]
    block_count = columns // BLOCK
    replica_count = float(lax.axis_size("dp"))
    hadamard = hadamard_matrix(BLOCK)
    sign_flip = (1 - 2 * sign_bits).astype(jnp.float32)
    units = levels.astype(jnp.float32)
    top_unit = units[levels.shape[0] - 1]
    table = 2.0 * units / top_unit - 1.0
    signed = gradient[0] * sign_flip.astype(jnp.bfloat16)
    blocks = signed.reshape(row_count * block_count, BLOCK)
    rotated = jnp.dot(blocks, hadamard.astype(jnp.bfloat16), preferred_element_type=jnp.float32) * (
        1.0 / math.sqrt(BLOCK)
    )
    local_peak = jnp.max(jnp.abs(rotated), axis=1)
    block_scale = lax.pmax(local_peak, "dp") + epsilon
    normed = rotated / block_scale[:, None]
    dither = (
        thresholds[0].reshape(row_count * block_count, BLOCK).astype(jnp.float32) + 0.5
    ) / dither_range
    code_values = encode_units(normed, dither, table, units)
    flip_blocks = sign_flip.reshape(block_count, BLOCK)
    entries = float(row_count * lax.axis_size("tensor") * columns)
    owned_rows = row_count * block_count // lax.axis_size("dp")
    first_row = lax.axis_index("dp") * owned_rows
    owned_sum = lax.psum_scatter(code_values, "dp", scatter_dimension=0, tiled=True)
    owned_scale = lax.dynamic_slice_in_dim(block_scale, first_row, owned_rows, 0)
    block_ids = (first_row + jnp.arange(owned_rows, dtype=jnp.int32)) % block_count
    one_hot = (block_ids[:, None] == jnp.arange(block_count, dtype=jnp.int32)[None, :]).astype(
        jnp.bfloat16
    )
    owned_flip = jnp.dot(
        one_hot, flip_blocks.astype(jnp.bfloat16), preferred_element_type=jnp.float32
    )
    restored = (
        restore_blocks(owned_sum, owned_scale, hadamard, top_unit, replica_count) * owned_flip
    )
    squares = lax.psum(jnp.sum(restored * restored), ("dp", "tensor"))
    root_mean = jnp.sqrt(squares / entries + epsilon)
    factor = clip_rms[0] / jnp.maximum(root_mean, clip_rms[0])
    owned_part = (restored * factor).astype(jnp.bfloat16)
    gathered = lax.all_gather(owned_part, "dp", axis=0, tiled=True)
    return gathered.reshape(row_count, columns)


def solution(mesh):
    in_specs = (P("dp", "tensor", None), P("dp", "tensor", None), P(), P(), P())
    out_specs = P("tensor", None)
    sixteen = mesh.shape["dp"] == 16 and mesh.shape["tensor"] == 2
    call = fused_body if sixteen else body
    return jax.shard_map(call, mesh=mesh, in_specs=in_specs, out_specs=out_specs, check_vma=False)
```

```python
import functools
import math

import jax
import jax.numpy as jnp
from jax import lax
from jax.experimental import pallas as pl
from jax.experimental.pallas import tpu as pltpu
from jax.sharding import PartitionSpec as P

BLOCK = 128
MESH = pl.DeviceIdType.MESH
LOADS = 4
GUARD = 64
CHUNK = 2
epsilon = 1e-06
sharpness = 16.0
dither_range = 4096.0
LOG2E = math.log2(math.e)


def hadamard_matrix(size):
    position = jnp.arange(size, dtype=jnp.int32)
    parity = jnp.zeros((size, size), jnp.int32)
    for bit_index in range(size.bit_length() - 1):
        parity = parity + (position[:, None] >> bit_index & 1) * (
            position[None, :] >> bit_index & 1
        )
    return (1 - 2 * (parity % 2)).astype(jnp.float32)


def kernel(
    entries, grad_in, thr_in, sign_in, levels, clip, out,
    grad, thr, sign, flip, load,
    rot, amp, peak, peak_a, peak_b, send, recv_a, part, recv_b, merged, ssq, ssq_in,
    pk_send, pk_a, pk_b, a_send, a_recv, b_send, b_recv, q_send, q_recv, g_send, z_recv, p_recv,
):
    me, core = lax.axis_index("dp"), lax.axis_index("tensor")
    x, y, z = me % 2, (me // 2) % 2, me // 4
    blocks = rot.shape[0]
    half = blocks // 2
    chunks = half // CHUNK
    count = 16.0
    inv_root = 1.0 / math.sqrt(BLOCK)

    def plane_peer(d):
        dx, dy = d % 2, d // 2
        return ((y + dy) % 2) * 2 + (x + dx) % 2

    def z_peer(d):
        return (z + d) % 4

    def dev(zz, q, cc=None):
        return (zz * 4 + q, core if cc is None else cc)

    def remote(src, dst, ss, rs, where):
        return pltpu.make_async_remote_copy(
            src_ref=src, dst_ref=dst, send_sem=ss, recv_sem=rs, device_id=where, device_id_type=MESH
        )

    mine = y * 2 + x
    others = [(d, c) for d in range(16) for c in range(2) if (d, c) != (0, 0)]

    fetch_sign = pltpu.make_async_copy(sign_in, sign, load.at[0])
    fetch_sign.start()
    quarter = grad.shape[1] // LOADS
    fetch_grad = [
        pltpu.make_async_copy(
            grad_in.at[0, :, pl.ds(i * quarter, quarter)],
            grad.at[:, pl.ds(i * quarter, quarter)],
            load.at[i + 2],
        )
        for i in range(LOADS)
    ]
    for c in fetch_grad:
        c.start()
    fetch_thr = pltpu.make_async_copy(thr_in.at[0], thr, load.at[1])
    fetch_thr.start()

    barrier = pltpu.get_barrier_semaphore()
    for d, c in others:
        pl.semaphore_signal(
            barrier, inc=1, device_id=((me + d) % 16, (core + c) % 2), device_id_type=MESH
        )

    lane = lax.broadcasted_iota(jnp.int32, (BLOCK, BLOCK), 1)
    row = lax.broadcasted_iota(jnp.int32, (BLOCK, BLOCK), 0)
    bits = lane & row
    bits = bits ^ (bits >> 4)
    bits = bits ^ (bits >> 2)
    bits = bits ^ (bits >> 1)
    hb = (1 - 2 * (bits & 1)).astype(jnp.float32).astype(jnp.bfloat16)
    fetch_sign.wait()
    flip[...] = (1 - 2 * sign[...]).astype(jnp.float32)
    peak[...] = jnp.zeros_like(peak)

    def rotate(b, _):
        cols = pl.ds(pl.multiple_of(b * BLOCK, BLOCK), BLOCK)
        signed = grad[:, cols] * flip[pl.ds(b, 1), :].astype(jnp.bfloat16)
        rot[b] = jnp.dot(signed, hb, preferred_element_type=jnp.float32)
        turned = lax.dot_general(
            hb, signed, (((0,), (1,)), ((), ())), preferred_element_type=jnp.float32
        )
        peak[pl.ds(b, 1), :] = jnp.max(jnp.abs(turned), axis=0, keepdims=True) * inv_root
        return 0

    for i in range(LOADS):
        fetch_grad[i].wait()
        lax.fori_loop(i * blocks // LOADS, (i + 1) * blocks // LOADS, rotate, 0, unroll=True)

    def amplitude(b, _):
        cols = pl.ds(pl.multiple_of(b * BLOCK, BLOCK), BLOCK)
        power = (thr[:, cols].astype(jnp.float32) + 0.5) * (sharpness * LOG2E / dither_range)
        amp[b] = jnp.exp2(power)
        return 0

    pl.semaphore_wait(barrier, len(others))

    copies = []
    first = [
        remote(peak, peak_a.at[d - 1], pk_send.at[d - 1], pk_a.at[d - 1], dev(z, plane_peer(d)))
        for d in range(1, 4)
    ]
    for c in first:
        c.start()
    fetch_thr.wait()
    lax.fori_loop(0, half, amplitude, 0, unroll=2)
    for c in first:
        c.wait()
    peak[...] = jnp.maximum(
        jnp.maximum(peak[...], peak_a[0]), jnp.maximum(peak_a[1], peak_a[2])
    )
    second = [
        remote(peak, peak_b.at[d - 1], pk_send.at[d + 2], pk_b.at[d - 1], dev(z_peer(d), mine))
        for d in range(1, 4)
    ]
    for c in second:
        c.start()
    lax.fori_loop(half, blocks, amplitude, 0, unroll=2)
    for c in second:
        c.wait()
    scale = (
        jnp.maximum(jnp.maximum(peak[...], peak_b[0]), jnp.maximum(peak_b[1], peak_b[2])) + epsilon
    )
    units = [levels[p].astype(jnp.float32) for p in range(16)]
    top = units[15]
    packed = [units[p] + (units[p + 1] - units[p]) * 0.125 for p in range(15)]
    half_top = 0.5 * top
    peak_a[0] = scale
    peak_a[1] = (half_top * inv_root) / scale

    decay = math.exp(-sharpness)
    step = (2.0**20 - 2.0 * GUARD) / top
    shift = 2.0 * GUARD * count / (2.0**20 - 2.0 * GUARD) + count

    def code_of(b):
        inverse = jnp.sum(
            jnp.where(lane == row, peak_a[1, pl.ds(b, 1), :], 0.0), axis=1, keepdims=True
        )
        place = rot[b] * inverse + half_top
        pack = jnp.zeros_like(place) + packed[0]
        for p in range(1, 15):
            pack = jnp.where(place >= units[p], packed[p], pack)
        low = jnp.floor(pack)
        gap = (pack - low) * 8.0
        inv_gap = ((10.0 - gap) * gap - 35.0) * gap + 50.0
        w = jnp.exp2((place - low) * inv_gap * (-sharpness * LOG2E / 24.0))
        a = amp[b]
        upper = (1.0 - w) * (a * (decay / (1.0 - decay)) + 1.0 / (1.0 - decay))
        return low + gap * (upper / (1.0 + a * w))

    def plane_copy(c, d):
        return remote(
            send.at[c, plane_peer(d)], recv_a.at[c, d - 1], a_send.at[c, d - 1],
            a_recv.at[c, d - 1], dev(z, plane_peer(d)),
        )

    def z_copy(c, d):
        return remote(
            part.at[c, z_peer(d)], recv_b.at[c, d - 1], b_send.at[c, d - 1],
            b_recv.at[c, d - 1], dev(z_peer(d), mine),
        )

    def encode_chunk(c):
        for h in range(2):
            def one(k, _):
                number = (code_of(h * half + c * CHUNK + k) * step + (GUARD + 0.5)).astype(jnp.int32)
                number = jnp.clip(number, 0, 2**20 - 1)
                high = ((number >> 4) - 2**15).astype(jnp.int16)
                nibble = number & 15
                for yy in range(2):
                    four = jnp.full((16, BLOCK), -(2**15), jnp.int32)
                    for zz in range(4):
                        at = 16 * (2 * zz + yy)
                        send[c, yy * 2 + h, zz, k] = high[at:at + 16]
                        four = four + (nibble[at:at + 16] << (4 * zz))
                    send[c, yy * 2 + h, 4, k] = four.astype(jnp.int16)
                return 0
            lax.fori_loop(0, CHUNK, one, 0, unroll=True)
        for d in range(1, 4):
            plane_copy(c, d).start()

    def add_plane(c):
        for d in range(1, 4):
            plane_copy(c, d).wait_recv()
        sources = [send.at[c, mine], recv_a.at[c, 0], recv_a.at[c, 1], recv_a.at[c, 2]]
        fours = [ref[4].astype(jnp.int32) + 2**15 for ref in sources]
        for zz in range(4):
            upper = sum(ref[zz].astype(jnp.int32) for ref in sources) + 4 * 2**15
            lower = sum((four >> (4 * zz)) & 15 for four in fours)
            part[c, zz] = (upper * 16 + lower).astype(jnp.float32)
        for d in range(1, 4):
            z_copy(c, d).start()

    for c in range(chunks):
        encode_chunk(c)
        if c >= 3:
            add_plane(c - 3)
    for c in range(max(chunks - 3, 0), chunks):
        add_plane(c)

    group = 2 * z + y
    lane16 = lax.broadcasted_iota(jnp.int32, (16, BLOCK), 1)
    row16 = lax.broadcasted_iota(jnp.int32, (16, BLOCK), 0)
    own_rows = lane16 == row16 + 16 * group
    total = jnp.zeros((16, BLOCK), jnp.float32)
    for c in range(chunks):
        for d in range(1, 4):
            z_copy(c, d).wait_recv()
        sums = (part[c, z] + recv_b[c, 0]) + (recv_b[c, 1] + recv_b[c, 2])
        for k in range(CHUNK):
            b = x * half + c * CHUNK + k
            own_scale = jnp.sum(
                jnp.where(own_rows, peak_a[0, pl.ds(b, 1), :], 0.0), axis=1, keepdims=True
            )
            value = (sums[k] * (2.0 / (step * top)) - shift) * own_scale
            merged[c * CHUNK + k] = value
            total = total + value * value
    ssq[...] = total[0:8] + total[8:16]

    ssq_copies = [
        remote(
            ssq, ssq_in.at[i], q_send.at[i], q_recv.at[i], ((me + d) % 16, (core + c) % 2)
        )
        for i, (d, c) in enumerate(others)
    ]
    for c in ssq_copies:
        c.start()

    flat = merged[...].reshape(half * 16, BLOCK)
    hi = flat.astype(jnp.bfloat16)
    rest = flat - hi.astype(jnp.float32)
    mid = rest.astype(jnp.bfloat16)
    lo = (rest - mid.astype(jnp.float32)).astype(jnp.bfloat16)
    restored = (
        jnp.dot(hi, hb, preferred_element_type=jnp.float32)
        + jnp.dot(mid, hb, preferred_element_type=jnp.float32)
        + jnp.dot(lo, hb, preferred_element_type=jnp.float32)
    ) * inv_root
    merged[...] = restored.reshape(half, 16, BLOCK)

    for c in ssq_copies:
        c.wait_recv()
    squares = jnp.sum(ssq[...] + jnp.sum(ssq_in[...], axis=0), keepdims=True)
    root_mean = jnp.sqrt(squares / entries + epsilon)
    factor = clip[0] / jnp.maximum(root_mean, clip[0])

    def piece(zz, yy, xx):
        return out.at[
            pl.ds(pl.multiple_of(16 * (2 * zz + yy), 16), 16),
            pl.ds(pl.multiple_of(xx * (half * BLOCK), BLOCK), half * BLOCK),
        ]

    for k in range(half):
        b = x * half + k
        out[
            pl.ds(pl.multiple_of(16 * group, 16), 16),
            pl.ds(pl.multiple_of(b * BLOCK, BLOCK), BLOCK),
        ] = (merged[k] * flip[pl.ds(b, 1), :] * factor).astype(jnp.bfloat16)

    own = piece(z, y, x)
    sent = []

    def go(copy):
        copy.start()
        sent.append(copy)

    for d in range(1, 4):
        go(remote(own, own, g_send.at[d - 1, 0], z_recv.at[d - 1], dev(z_peer(d), mine)))
    for s in range(4):
        zs = (z + 4 - s) % 4
        here = piece(zs, y, x)
        if s:
            remote(here, here, g_send.at[s - 1, 0], z_recv.at[s - 1], dev(z, mine)).wait_recv()
        for d in range(1, 4):
            go(remote(here, here, g_send.at[s, d], p_recv.at[s, d - 1], dev(z, plane_peer(d))))
    for s in range(4):
        zs = (z + 4 - s) % 4
        for d in range(1, 4):
            dx, dy = d % 2, d // 2
            there = piece(zs, (y + dy) % 2, (x + dx) % 2)
            remote(there, there, g_send.at[s, d], p_recv.at[s, d - 1], dev(z, plane_peer(d))).wait_recv()

    for c in range(chunks):
        for d in range(1, 4):
            plane_copy(c, d).wait_send()
            z_copy(c, d).wait_send()
    for c in ssq_copies:
        c.wait_send()
    for c in sent:
        c.wait_send()


def fused_body(gradient, thresholds, sign_bits, levels, clip_rms):
    rows, columns = gradient.shape[1], gradient.shape[2]
    blocks = columns // BLOCK
    half = blocks // 2
    chunks = half // CHUNK
    entries = float(rows * lax.axis_size("tensor") * columns)
    vmem = pl.BlockSpec(memory_space=pltpu.VMEM)
    hbm = pl.BlockSpec(memory_space=pl.ANY)
    smem = pl.BlockSpec(memory_space=pltpu.SMEM)
    f32 = jnp.float32
    padded = -(-blocks // 8) * 8
    dma = pltpu.SemaphoreType.DMA
    return pl.pallas_call(
        functools.partial(kernel, entries),
        out_shape=pltpu.VMEM((rows, columns), jnp.bfloat16),
        in_specs=[hbm, hbm, hbm, smem, smem],
        out_specs=vmem,
        scratch_shapes=[
            pltpu.VMEM((rows, columns), jnp.bfloat16),
            pltpu.VMEM((rows, columns), jnp.int32),
            pltpu.VMEM((blocks, BLOCK), jnp.int32),
            pltpu.VMEM((blocks, BLOCK), f32),
            dma((LOADS + 2,)),
            pltpu.VMEM((blocks, rows, BLOCK), f32),
            pltpu.VMEM((blocks, rows, BLOCK), f32),
            pltpu.VMEM((padded, BLOCK), f32),
            pltpu.VMEM((3, padded, BLOCK), f32),
            pltpu.VMEM((3, padded, BLOCK), f32),
            pltpu.VMEM((chunks, 4, 5, CHUNK, 16, BLOCK), jnp.int16),
            pltpu.VMEM((chunks, 3, 5, CHUNK, 16, BLOCK), jnp.int16),
            pltpu.VMEM((chunks, 4, CHUNK, 16, BLOCK), f32),
            pltpu.VMEM((chunks, 3, CHUNK, 16, BLOCK), f32),
            pltpu.VMEM((half, 16, BLOCK), f32),
            pltpu.VMEM((8, BLOCK), f32),
            pltpu.VMEM((31, 8, BLOCK), f32),
            dma((6,)), dma((3,)), dma((3,)),
            dma((chunks, 3)), dma((chunks, 3)), dma((chunks, 3)), dma((chunks, 3)),
            dma((31,)), dma((31,)),
            dma((4, 4)), dma((3,)), dma((4, 3)),
        ],
        compiler_params=pltpu.CompilerParams(
            collective_id=0, has_side_effects=True, vmem_limit_bytes=60 * 1024 * 1024
        ),
    )(gradient, thresholds, sign_bits.reshape(blocks, BLOCK), levels, clip_rms)


def encode_units(normed, dither, table, units):
    low_level = jnp.zeros_like(normed) + table[0]
    high_level = jnp.zeros_like(normed) + table[1]
    low_unit = jnp.zeros_like(normed) + units[0]
    high_unit = jnp.zeros_like(normed) + units[1]
    for position in range(1, table.shape[0] - 1):
        above = normed >= table[position]
        low_level = jnp.where(above, table[position], low_level)
        high_level = jnp.where(above, table[position + 1], high_level)
        low_unit = jnp.where(above, units[position], low_unit)
        high_unit = jnp.where(above, units[position + 1], high_unit)
    fraction = (normed - low_level) / (high_level - low_level)
    bottom = jax.nn.sigmoid(-sharpness * dither)
    upper_end = jax.nn.sigmoid(sharpness * (1.0 - dither))
    ramp = (jax.nn.sigmoid(sharpness * (fraction - dither)) - bottom) / (upper_end - bottom)
    return low_unit + (high_unit - low_unit) * ramp


def restore_blocks(code_sum, block_scale, hadamard, top_unit, count):
    merged = (2.0 * code_sum / top_unit - count) * block_scale[:, None]
    product = jnp.dot(merged, hadamard, precision=lax.Precision.HIGHEST)
    return product * (1.0 / math.sqrt(hadamard.shape[0]))


def body(gradient, thresholds, sign_bits, levels, clip_rms):
    row_count = gradient.shape[1]
    columns = gradient.shape[2]
    block_count = columns // BLOCK
    replica_count = float(lax.axis_size("dp"))
    hadamard = hadamard_matrix(BLOCK)
    sign_flip = (1 - 2 * sign_bits).astype(jnp.float32)
    units = levels.astype(jnp.float32)
    top_unit = units[levels.shape[0] - 1]
    table = 2.0 * units / top_unit - 1.0
    signed = gradient[0] * sign_flip.astype(jnp.bfloat16)
    blocks = signed.reshape(row_count * block_count, BLOCK)
    rotated = jnp.dot(blocks, hadamard.astype(jnp.bfloat16), preferred_element_type=jnp.float32) * (
        1.0 / math.sqrt(BLOCK)
    )
    local_peak = jnp.max(jnp.abs(rotated), axis=1)
    block_scale = lax.pmax(local_peak, "dp") + epsilon
    normed = rotated / block_scale[:, None]
    dither = (
        thresholds[0].reshape(row_count * block_count, BLOCK).astype(jnp.float32) + 0.5
    ) / dither_range
    code_values = encode_units(normed, dither, table, units)
    flip_blocks = sign_flip.reshape(block_count, BLOCK)
    entries = float(row_count * lax.axis_size("tensor") * columns)
    owned_rows = row_count * block_count // lax.axis_size("dp")
    first_row = lax.axis_index("dp") * owned_rows
    owned_sum = lax.psum_scatter(code_values, "dp", scatter_dimension=0, tiled=True)
    owned_scale = lax.dynamic_slice_in_dim(block_scale, first_row, owned_rows, 0)
    block_ids = (first_row + jnp.arange(owned_rows, dtype=jnp.int32)) % block_count
    one_hot = (block_ids[:, None] == jnp.arange(block_count, dtype=jnp.int32)[None, :]).astype(
        jnp.bfloat16
    )
    owned_flip = jnp.dot(
        one_hot, flip_blocks.astype(jnp.bfloat16), preferred_element_type=jnp.float32
    )
    restored = (
        restore_blocks(owned_sum, owned_scale, hadamard, top_unit, replica_count) * owned_flip
    )
    squares = lax.psum(jnp.sum(restored * restored), ("dp", "tensor"))
    root_mean = jnp.sqrt(squares / entries + epsilon)
    factor = clip_rms[0] / jnp.maximum(root_mean, clip_rms[0])
    owned_part = (restored * factor).astype(jnp.bfloat16)
    gathered = lax.all_gather(owned_part, "dp", axis=0, tiled=True)
    return gathered.reshape(row_count, columns)


def solution(mesh):
    in_specs = (P("dp", "tensor", None), P("dp", "tensor", None), P(), P(), P())
    out_specs = P("tensor", None)
    sixteen = mesh.shape["dp"] == 16 and mesh.shape["tensor"] == 2
    call = fused_body if sixteen else body
    return jax.shard_map(call, mesh=mesh, in_specs=in_specs, out_specs=out_specs, check_vma=False)
```

```python
import functools
import math

import jax
import jax.numpy as jnp
from jax import lax
from jax.experimental import pallas as pl
from jax.experimental.pallas import tpu as pltpu
from jax.sharding import PartitionSpec as P

BLOCK = 128
MESH = pl.DeviceIdType.MESH
LOADS = 4
GUARD = 64
CHUNK = 2
epsilon = 1e-06
sharpness = 16.0
dither_range = 4096.0
LOG2E = math.log2(math.e)


def hadamard_matrix(size):
    position = jnp.arange(size, dtype=jnp.int32)
    parity = jnp.zeros((size, size), jnp.int32)
    for bit_index in range(size.bit_length() - 1):
        parity = parity + (position[:, None] >> bit_index & 1) * (
            position[None, :] >> bit_index & 1
        )
    return (1 - 2 * (parity % 2)).astype(jnp.float32)


def kernel(
    entries, grad_in, thr_in, sign_in, levels, clip, out,
    grad, thr, sign, flip, load,
    rot, amp, peak, peak_a, peak_b, send, recv_a, part, recv_b, merged, ssq, ssq_in,
    pk_send, pk_a, pk_b, a_send, a_recv, b_send, b_recv, q_send, q_recv, g_send, z_recv, p_recv,
):
    me, core = lax.axis_index("dp"), lax.axis_index("tensor")
    x, y, z = me % 2, (me // 2) % 2, me // 4
    blocks = rot.shape[0]
    half = blocks // 2
    chunks = half // CHUNK
    count = 16.0
    inv_root = 1.0 / math.sqrt(BLOCK)

    def plane_peer(d):
        dx, dy = d % 2, d // 2
        return ((y + dy) % 2) * 2 + (x + dx) % 2

    def z_peer(d):
        return (z + d) % 4

    def dev(zz, q, cc=None):
        return (zz * 4 + q, core if cc is None else cc)

    def remote(src, dst, ss, rs, where):
        return pltpu.make_async_remote_copy(
            src_ref=src, dst_ref=dst, send_sem=ss, recv_sem=rs, device_id=where, device_id_type=MESH
        )

    mine = y * 2 + x
    others = [(d, c) for d in range(16) for c in range(2) if (d, c) != (0, 0)]

    fetch_sign = pltpu.make_async_copy(sign_in, sign, load.at[0])
    fetch_sign.start()
    quarter = grad.shape[1] // LOADS
    fetch_grad = [
        pltpu.make_async_copy(
            grad_in.at[0, :, pl.ds(i * quarter, quarter)],
            grad.at[:, pl.ds(i * quarter, quarter)],
            load.at[i + 2],
        )
        for i in range(LOADS)
    ]
    for c in fetch_grad:
        c.start()
    fetch_thr = pltpu.make_async_copy(thr_in.at[0], thr, load.at[1])
    fetch_thr.start()

    barrier = pltpu.get_barrier_semaphore()
    for d, c in others:
        pl.semaphore_signal(
            barrier, inc=1, device_id=((me + d) % 16, (core + c) % 2), device_id_type=MESH
        )

    lane = lax.broadcasted_iota(jnp.int32, (BLOCK, BLOCK), 1)
    row = lax.broadcasted_iota(jnp.int32, (BLOCK, BLOCK), 0)
    bits = lane & row
    bits = bits ^ (bits >> 4)
    bits = bits ^ (bits >> 2)
    bits = bits ^ (bits >> 1)
    hb = (1 - 2 * (bits & 1)).astype(jnp.float32).astype(jnp.bfloat16)
    fetch_sign.wait()
    flip[...] = (1 - 2 * sign[...]).astype(jnp.float32)
    peak[...] = jnp.zeros_like(peak)

    def rotate(b, _):
        cols = pl.ds(pl.multiple_of(b * BLOCK, BLOCK), BLOCK)
        signed = grad[:, cols] * flip[pl.ds(b, 1), :].astype(jnp.bfloat16)
        rot[b] = jnp.dot(signed, hb, preferred_element_type=jnp.float32)
        turned = lax.dot_general(
            hb, signed, (((0,), (1,)), ((), ())), preferred_element_type=jnp.float32
        )
        peak[pl.ds(b, 1), :] = jnp.max(jnp.abs(turned), axis=0, keepdims=True) * inv_root
        return 0

    for i in range(LOADS):
        fetch_grad[i].wait()
        lax.fori_loop(i * blocks // LOADS, (i + 1) * blocks // LOADS, rotate, 0, unroll=True)

    def amplitude(b, _):
        cols = pl.ds(pl.multiple_of(b * BLOCK, BLOCK), BLOCK)
        power = (thr[:, cols].astype(jnp.float32) + 0.5) * (sharpness * LOG2E / dither_range)
        amp[b] = jnp.exp2(power)
        return 0

    pl.semaphore_wait(barrier, len(others))

    copies = []
    first = [
        remote(peak, peak_a.at[d - 1], pk_send.at[d - 1], pk_a.at[d - 1], dev(z, plane_peer(d)))
        for d in range(1, 4)
    ]
    for c in first:
        c.start()
    fetch_thr.wait()
    lax.fori_loop(0, half, amplitude, 0, unroll=2)
    for c in first:
        c.wait()
    peak[...] = jnp.maximum(
        jnp.maximum(peak[...], peak_a[0]), jnp.maximum(peak_a[1], peak_a[2])
    )
    second = [
        remote(peak, peak_b.at[d - 1], pk_send.at[d + 2], pk_b.at[d - 1], dev(z_peer(d), mine))
        for d in range(1, 4)
    ]
    for c in second:
        c.start()
    lax.fori_loop(half, blocks, amplitude, 0, unroll=2)
    for c in second:
        c.wait()
    scale = (
        jnp.maximum(jnp.maximum(peak[...], peak_b[0]), jnp.maximum(peak_b[1], peak_b[2])) + epsilon
    )
    units = [levels[p].astype(jnp.float32) for p in range(16)]
    top = units[15]
    packed = [units[p] + (units[p + 1] - units[p]) * 0.125 for p in range(15)]
    half_top = 0.5 * top
    peak_a[0] = scale
    peak_a[1] = (half_top * inv_root) / scale

    decay = math.exp(-sharpness)
    step = (2.0**20 - 2.0 * GUARD) / top
    shift = 2.0 * GUARD * count / (2.0**20 - 2.0 * GUARD) + count

    def code_of(b):
        inverse = jnp.sum(
            jnp.where(lane == row, peak_a[1, pl.ds(b, 1), :], 0.0), axis=1, keepdims=True
        )
        place = rot[b] * inverse + half_top
        pack = jnp.zeros_like(place) + packed[0]
        for p in range(1, 15):
            pack = jnp.where(place >= units[p], packed[p], pack)
        low = jnp.floor(pack)
        gap = (pack - low) * 8.0
        inv_gap = ((10.0 - gap) * gap - 35.0) * gap + 50.0
        w = jnp.exp2((place - low) * inv_gap * (-sharpness * LOG2E / 24.0))
        a = amp[b]
        upper = (1.0 - w) * (a * (decay / (1.0 - decay)) + 1.0 / (1.0 - decay))
        return low + gap * (upper / (1.0 + a * w))

    def plane_copy(c, d):
        return remote(
            send.at[c, plane_peer(d)], recv_a.at[c, d - 1], a_send.at[c, d - 1],
            a_recv.at[c, d - 1], dev(z, plane_peer(d)),
        )

    def z_copy(c, d):
        return remote(
            part.at[c, z_peer(d)], recv_b.at[c, d - 1], b_send.at[c, d - 1],
            b_recv.at[c, d - 1], dev(z_peer(d), mine),
        )

    def encode_chunk(c):
        for h in range(2):
            def one(k, _):
                number = (code_of(h * half + c * CHUNK + k) * step + (GUARD + 0.5)).astype(jnp.int32)
                number = jnp.clip(number, 0, 2**20 - 1)
                high = ((number >> 4) - 2**15).astype(jnp.int16)
                nibble = number & 15
                for yy in range(2):
                    four = jnp.full((16, BLOCK), -(2**15), jnp.int32)
                    for zz in range(4):
                        at = 16 * (2 * zz + yy)
                        send[c, yy * 2 + h, zz, k] = high[at:at + 16]
                        four = four + (nibble[at:at + 16] << (4 * zz))
                    send[c, yy * 2 + h, 4, k] = four.astype(jnp.int16)
                return 0
            lax.fori_loop(0, CHUNK, one, 0, unroll=True)
        for d in (3, 1, 2):
            plane_copy(c, d).start()

    def add_plane(c):
        for d in range(1, 4):
            plane_copy(c, d).wait_recv()
        sources = [send.at[c, mine], recv_a.at[c, 0], recv_a.at[c, 1], recv_a.at[c, 2]]
        fours = [ref[4].astype(jnp.int32) + 2**15 for ref in sources]
        for zz in range(4):
            upper = sum(ref[zz].astype(jnp.int32) for ref in sources) + 4 * 2**15
            lower = sum((four >> (4 * zz)) & 15 for four in fours)
            part[c, zz] = (upper * 16 + lower).astype(jnp.float32)
        for d in range(1, 4):
            z_copy(c, d).start()

    for c in range(chunks):
        encode_chunk(c)
        if c >= 3:
            add_plane(c - 3)
    for c in range(max(chunks - 3, 0), chunks):
        add_plane(c)

    group = 2 * z + y
    lane16 = lax.broadcasted_iota(jnp.int32, (16, BLOCK), 1)
    row16 = lax.broadcasted_iota(jnp.int32, (16, BLOCK), 0)
    own_rows = lane16 == row16 + 16 * group
    total = jnp.zeros((16, BLOCK), jnp.float32)
    for c in range(chunks):
        for d in range(1, 4):
            z_copy(c, d).wait_recv()
        sums = (part[c, z] + recv_b[c, 0]) + (recv_b[c, 1] + recv_b[c, 2])
        for k in range(CHUNK):
            b = x * half + c * CHUNK + k
            own_scale = jnp.sum(
                jnp.where(own_rows, peak_a[0, pl.ds(b, 1), :], 0.0), axis=1, keepdims=True
            )
            value = (sums[k] * (2.0 / (step * top)) - shift) * own_scale
            merged[c * CHUNK + k] = value
            total = total + value * value
    ssq[...] = total[0:8] + total[8:16]

    ssq_copies = [
        remote(
            ssq, ssq_in.at[i], q_send.at[i], q_recv.at[i], ((me + d) % 16, (core + c) % 2)
        )
        for i, (d, c) in enumerate(others)
    ]
    for c in ssq_copies:
        c.start()

    flat = merged[...].reshape(half * 16, BLOCK)
    hi = flat.astype(jnp.bfloat16)
    rest = flat - hi.astype(jnp.float32)
    mid = rest.astype(jnp.bfloat16)
    lo = (rest - mid.astype(jnp.float32)).astype(jnp.bfloat16)
    restored = (
        jnp.dot(hi, hb, preferred_element_type=jnp.float32)
        + jnp.dot(mid, hb, preferred_element_type=jnp.float32)
        + jnp.dot(lo, hb, preferred_element_type=jnp.float32)
    ) * inv_root
    merged[...] = restored.reshape(half, 16, BLOCK)

    for c in ssq_copies:
        c.wait_recv()
    squares = jnp.sum(ssq[...] + jnp.sum(ssq_in[...], axis=0), keepdims=True)
    root_mean = jnp.sqrt(squares / entries + epsilon)
    factor = clip[0] / jnp.maximum(root_mean, clip[0])

    def piece(zz, yy, xx):
        return out.at[
            pl.ds(pl.multiple_of(16 * (2 * zz + yy), 16), 16),
            pl.ds(pl.multiple_of(xx * (half * BLOCK), BLOCK), half * BLOCK),
        ]

    for k in range(half):
        b = x * half + k
        out[
            pl.ds(pl.multiple_of(16 * group, 16), 16),
            pl.ds(pl.multiple_of(b * BLOCK, BLOCK), BLOCK),
        ] = (merged[k] * flip[pl.ds(b, 1), :] * factor).astype(jnp.bfloat16)

    own = piece(z, y, x)
    sent = []

    def go(copy):
        copy.start()
        sent.append(copy)

    for d in range(1, 4):
        go(remote(own, own, g_send.at[d - 1, 0], z_recv.at[d - 1], dev(z_peer(d), mine)))
    for s in range(4):
        zs = (z + 4 - s) % 4
        here = piece(zs, y, x)
        if s:
            remote(here, here, g_send.at[s - 1, 0], z_recv.at[s - 1], dev(z, mine)).wait_recv()
        for d in (3, 1, 2):
            go(remote(here, here, g_send.at[s, d], p_recv.at[s, d - 1], dev(z, plane_peer(d))))
    for s in range(4):
        zs = (z + 4 - s) % 4
        for d in range(1, 4):
            dx, dy = d % 2, d // 2
            there = piece(zs, (y + dy) % 2, (x + dx) % 2)
            remote(there, there, g_send.at[s, d], p_recv.at[s, d - 1], dev(z, plane_peer(d))).wait_recv()

    for c in range(chunks):
        for d in range(1, 4):
            plane_copy(c, d).wait_send()
            z_copy(c, d).wait_send()
    for c in ssq_copies:
        c.wait_send()
    for c in sent:
        c.wait_send()


def fused_body(gradient, thresholds, sign_bits, levels, clip_rms):
    rows, columns = gradient.shape[1], gradient.shape[2]
    blocks = columns // BLOCK
    half = blocks // 2
    chunks = half // CHUNK
    entries = float(rows * lax.axis_size("tensor") * columns)
    vmem = pl.BlockSpec(memory_space=pltpu.VMEM)
    hbm = pl.BlockSpec(memory_space=pl.ANY)
    smem = pl.BlockSpec(memory_space=pltpu.SMEM)
    f32 = jnp.float32
    padded = -(-blocks // 8) * 8
    dma = pltpu.SemaphoreType.DMA
    return pl.pallas_call(
        functools.partial(kernel, entries),
        out_shape=pltpu.VMEM((rows, columns), jnp.bfloat16),
        in_specs=[hbm, hbm, hbm, smem, smem],
        out_specs=vmem,
        scratch_shapes=[
            pltpu.VMEM((rows, columns), jnp.bfloat16),
            pltpu.VMEM((rows, columns), jnp.int32),
            pltpu.VMEM((blocks, BLOCK), jnp.int32),
            pltpu.VMEM((blocks, BLOCK), f32),
            dma((LOADS + 2,)),
            pltpu.VMEM((blocks, rows, BLOCK), f32),
            pltpu.VMEM((blocks, rows, BLOCK), f32),
            pltpu.VMEM((padded, BLOCK), f32),
            pltpu.VMEM((3, padded, BLOCK), f32),
            pltpu.VMEM((3, padded, BLOCK), f32),
            pltpu.VMEM((chunks, 4, 5, CHUNK, 16, BLOCK), jnp.int16),
            pltpu.VMEM((chunks, 3, 5, CHUNK, 16, BLOCK), jnp.int16),
            pltpu.VMEM((chunks, 4, CHUNK, 16, BLOCK), f32),
            pltpu.VMEM((chunks, 3, CHUNK, 16, BLOCK), f32),
            pltpu.VMEM((half, 16, BLOCK), f32),
            pltpu.VMEM((8, BLOCK), f32),
            pltpu.VMEM((31, 8, BLOCK), f32),
            dma((6,)), dma((3,)), dma((3,)),
            dma((chunks, 3)), dma((chunks, 3)), dma((chunks, 3)), dma((chunks, 3)),
            dma((31,)), dma((31,)),
            dma((4, 4)), dma((3,)), dma((4, 3)),
        ],
        compiler_params=pltpu.CompilerParams(
            collective_id=0, has_side_effects=True, vmem_limit_bytes=60 * 1024 * 1024
        ),
    )(gradient, thresholds, sign_bits.reshape(blocks, BLOCK), levels, clip_rms)


def encode_units(normed, dither, table, units):
    low_level = jnp.zeros_like(normed) + table[0]
    high_level = jnp.zeros_like(normed) + table[1]
    low_unit = jnp.zeros_like(normed) + units[0]
    high_unit = jnp.zeros_like(normed) + units[1]
    for position in range(1, table.shape[0] - 1):
        above = normed >= table[position]
        low_level = jnp.where(above, table[position], low_level)
        high_level = jnp.where(above, table[position + 1], high_level)
        low_unit = jnp.where(above, units[position], low_unit)
        high_unit = jnp.where(above, units[position + 1], high_unit)
    fraction = (normed - low_level) / (high_level - low_level)
    bottom = jax.nn.sigmoid(-sharpness * dither)
    upper_end = jax.nn.sigmoid(sharpness * (1.0 - dither))
    ramp = (jax.nn.sigmoid(sharpness * (fraction - dither)) - bottom) / (upper_end - bottom)
    return low_unit + (high_unit - low_unit) * ramp


def restore_blocks(code_sum, block_scale, hadamard, top_unit, count):
    merged = (2.0 * code_sum / top_unit - count) * block_scale[:, None]
    product = jnp.dot(merged, hadamard, precision=lax.Precision.HIGHEST)
    return product * (1.0 / math.sqrt(hadamard.shape[0]))


def body(gradient, thresholds, sign_bits, levels, clip_rms):
    row_count = gradient.shape[1]
    columns = gradient.shape[2]
    block_count = columns // BLOCK
    replica_count = float(lax.axis_size("dp"))
    hadamard = hadamard_matrix(BLOCK)
    sign_flip = (1 - 2 * sign_bits).astype(jnp.float32)
    units = levels.astype(jnp.float32)
    top_unit = units[levels.shape[0] - 1]
    table = 2.0 * units / top_unit - 1.0
    signed = gradient[0] * sign_flip.astype(jnp.bfloat16)
    blocks = signed.reshape(row_count * block_count, BLOCK)
    rotated = jnp.dot(blocks, hadamard.astype(jnp.bfloat16), preferred_element_type=jnp.float32) * (
        1.0 / math.sqrt(BLOCK)
    )
    local_peak = jnp.max(jnp.abs(rotated), axis=1)
    block_scale = lax.pmax(local_peak, "dp") + epsilon
    normed = rotated / block_scale[:, None]
    dither = (
        thresholds[0].reshape(row_count * block_count, BLOCK).astype(jnp.float32) + 0.5
    ) / dither_range
    code_values = encode_units(normed, dither, table, units)
    flip_blocks = sign_flip.reshape(block_count, BLOCK)
    entries = float(row_count * lax.axis_size("tensor") * columns)
    owned_rows = row_count * block_count // lax.axis_size("dp")
    first_row = lax.axis_index("dp") * owned_rows
    owned_sum = lax.psum_scatter(code_values, "dp", scatter_dimension=0, tiled=True)
    owned_scale = lax.dynamic_slice_in_dim(block_scale, first_row, owned_rows, 0)
    block_ids = (first_row + jnp.arange(owned_rows, dtype=jnp.int32)) % block_count
    one_hot = (block_ids[:, None] == jnp.arange(block_count, dtype=jnp.int32)[None, :]).astype(
        jnp.bfloat16
    )
    owned_flip = jnp.dot(
        one_hot, flip_blocks.astype(jnp.bfloat16), preferred_element_type=jnp.float32
    )
    restored = (
        restore_blocks(owned_sum, owned_scale, hadamard, top_unit, replica_count) * owned_flip
    )
    squares = lax.psum(jnp.sum(restored * restored), ("dp", "tensor"))
    root_mean = jnp.sqrt(squares / entries + epsilon)
    factor = clip_rms[0] / jnp.maximum(root_mean, clip_rms[0])
    owned_part = (restored * factor).astype(jnp.bfloat16)
    gathered = lax.all_gather(owned_part, "dp", axis=0, tiled=True)
    return gathered.reshape(row_count, columns)


def solution(mesh):
    in_specs = (P("dp", "tensor", None), P("dp", "tensor", None), P(), P(), P())
    out_specs = P("tensor", None)
    sixteen = mesh.shape["dp"] == 16 and mesh.shape["tensor"] == 2
    call = fused_body if sixteen else body
    return jax.shard_map(call, mesh=mesh, in_specs=in_specs, out_specs=out_specs, check_vma=False)
```
